128 devices in a mesh: phase: 4 (over z), gz: 8 (over x_lo, y), gy: 4 (over x_hi, core).
Axes of the slice: x: 4 (x_hi: 2, x_lo: 2; x = x_hi * 2 + x_lo), y: 4, z: 4, core: 2. Of those that a mesh axis runs over, the one named last changes fastest.
Arguments:
- volume: bfloat16 [8, 64, 256, 512], P('phase', None, 'gz', 'gy'), may hold values from -6 to 6
- shift_code: int32 [8, 8, 4, 64], P('phase', 'gz', 'gy'), may hold values from 0 to 26, as said below
- frac_code: int32 [8, 8, 4, 64], P('phase', 'gz', 'gy'), may hold values from 0 to 63
- stencil: float32 [4], replicated, may hold values from 0.1 to 0.6
Outputs:
- prior_gradient: float32 [8, 64, 256, 512], P('phase', None, 'gz', 'gy')
The draws below stay inside these ranges and needn't reach their ends.
Inputs may be any that keep to these rules, and one draw needn't show every extreme that they name: `shift_code`: in every phase and region some block has the displacement (1, 1, 1) and another (-1, -1, -1); most displacement components are 0 or 1 in size.
All inputs are finite; a program needn't handle non-finite values.
Results may differ from the reference program's by a relative error of at most 0.00075.
Values may be sent and summed in bfloat16 or wider, within the bound.
No kernel may reach another device: no remote copies, remote signals or barrier semaphores. Data moves between devices by JAX's collectives and lax.ppermute only.
A program may use at most 256 MiB of HBM per device.

```python
import jax
import jax.numpy as jnp
from jax import lax

BS = 16
XC = 64
ZC = 32
YC = 128
REACH = 1
PHASES = 8
NZ = 256
NY = 512
BLK = 64
N_GZ = 8
N_GY = 4


def draw_shift_code(key, part):
    uniform_level = jax.random.randint(jax.random.fold_in(key, 505), (PHASES, N_GZ, N_GY, BLK, 3), 0, 16)
    delta = jnp.where(uniform_level < 6, 0, jnp.where(uniform_level < 10, 1, jnp.where(uniform_level < 14, -1, jnp.where(uniform_level == 14, REACH, -REACH))))
    delta = delta.at[:, :, :, 0, :].set(REACH)
    delta = delta.at[:, :, :, 1, :].set(-REACH)
    side = 2 * REACH + 1
    code = ((delta[..., 0] + REACH) * side + delta[..., 1] + REACH) * side + delta[..., 2] + REACH
    return code.astype(jnp.int32)


def set_ends(array, own_key, low, high):
    place = [jax.random.randint(jax.random.fold_in(own_key, axis), (), 0, length) for axis, length in enumerate(array.shape)]
    main_axis = array.shape.index(max(array.shape))
    neighbour = place[:main_axis] + [(place[main_axis] + 1) % array.shape[main_axis]] + place[main_axis + 1:]
    return array.at[tuple(place)].set(low).at[tuple(neighbour)].set(high)


def steps_of(stream_key, shape, pieces, least, high):
    factor_of = 1.0
    for dim, parts in pieces:
        draws = jax.random.uniform(jax.random.fold_in(jax.random.fold_in(stream_key, 6), dim), (parts,), jnp.float32, least / len(pieces), high / len(pieces))
        factor_of = factor_of * jnp.repeat(jnp.exp(draws), shape[dim] // parts).reshape((-1,) + (1,) * (len(shape) - 1 - dim))
    return factor_of


def bell_draw(key, extent, deviation, reach, shards=(), held_as=jnp.bfloat16):
    values = deviation * jax.random.normal(key, extent, jnp.float32)
    if shards:
        values = values * steps_of(key, extent, shards, -0.22, 0.18)
    return jnp.clip(values, -reach, reach).astype(held_as)


def setup_inputs(seed: int = 0) -> dict:
    key_list = jax.random.split(jax.random.key(seed), 5)
    volume = bell_draw(key_list[0], (PHASES, XC, NZ, NY), 1.0, 6.0, ((0, 4), (2, 8), (3, 4)))
    shift_code = draw_shift_code(jax.random.fold_in(key_list[4], 71), 0)
    frac_code = set_ends(jax.random.randint(key_list[2], (PHASES, N_GZ, N_GY, BLK), 0, 64), jax.random.fold_in(key_list[2], 1), 0, 63).astype(jnp.int32)
    stencil = jnp.clip(jax.random.uniform(key_list[3], (4,), jnp.float32, 0.1, 0.6), 0.1, 0.6)
    return {"volume": volume, "shift_code": shift_code, "frac_code": frac_code, "stencil": stencil}


def fraction_table():
    code_range = jnp.arange(64)
    levels = jnp.stack([code_range // 16 + 1, code_range // 4 % 4 + 1, code_range % 4 + 1], axis=1)
    return levels.astype(jnp.float32) / 5.0


def block_matrices(code_list, block_edge):
    onehot = (code_list[:, None] == jnp.arange(64)[None, :]).astype(jnp.float32)
    fractions = jnp.dot(onehot, fraction_table(), precision=lax.Precision.HIGHEST)
    position = jnp.arange(block_edge)
    identity = (position[:, None] == position[None, :]).astype(jnp.float32)
    forward_shift = (jnp.minimum(position + 1, block_edge - 1)[:, None] == position[None, :]).astype(jnp.float32)
    return (1.0 - fractions)[:, :, None, None] * identity + fractions[:, :, None, None] * forward_shift


def warp_blocks(source, matrices):
    along_first = jnp.einsum("nai,nijk->najk", matrices[:, 0], source, precision=lax.Precision.HIGHEST)
    second = jnp.einsum("nbj,najk->nabk", matrices[:, 1], along_first, precision=lax.Precision.HIGHEST)
    return jnp.einsum("nck,nabk->nabc", matrices[:, 2], second, precision=lax.Precision.HIGHEST)


def adjoint_blocks(source, matrices):
    along_first = jnp.einsum("nia,nijk->najk", matrices[:, 0], source, precision=lax.Precision.HIGHEST)
    second = jnp.einsum("njb,najk->nabk", matrices[:, 1], along_first, precision=lax.Precision.HIGHEST)
    return jnp.einsum("nkc,nabk->nabc", matrices[:, 2], second, precision=lax.Precision.HIGHEST)


def smooth(padded, stencil):
    center = padded[..., 1:-1, 1:-1, 1:-1]
    along_x = padded[..., 2:, 1:-1, 1:-1] + padded[..., :-2, 1:-1, 1:-1]
    along_z = padded[..., 1:-1, 2:, 1:-1] + padded[..., 1:-1, :-2, 1:-1]
    along_y = padded[..., 1:-1, 1:-1, 2:] + padded[..., 1:-1, 1:-1, :-2]
    return stencil[0] * center + stencil[1] * along_x + stencil[2] * along_z + stencil[3] * along_y


def volume_blocks(phase_volume):
    shaped = phase_volume.reshape(XC // BS, BS, N_GZ, ZC // BS, BS, N_GY, YC // BS, BS)
    return shaped.transpose(2, 5, 0, 3, 6, 1, 4, 7).reshape(-1, BS, BS, BS)


def block_volume(blocks):
    shaped = blocks.reshape(N_GZ, N_GY, XC // BS, ZC // BS, YC // BS, BS, BS, BS)
    return shaped.transpose(2, 5, 0, 3, 6, 1, 4, 7).reshape(XC, NZ, NY)


def source_index(codes):
    x_blocks = XC // BS
    z_blocks = ZC // BS
    y_blocks = YC // BS
    side = 2 * REACH + 1
    codes = codes.reshape(N_GZ, N_GY, BLK).astype(jnp.int32)
    local = jnp.arange(BLK).astype(jnp.int32)
    block_x = local // (z_blocks * y_blocks)
    block_z = local // y_blocks % z_blocks
    block_y = local % y_blocks
    region_z = jnp.arange(N_GZ).astype(jnp.int32)[:, None, None]
    region_y = jnp.arange(N_GY).astype(jnp.int32)[None, :, None]
    delta_x = codes // (side * side) - REACH
    delta_z = codes // side % side - REACH
    delta_y = codes % side - REACH
    source_x = jnp.clip(block_x + delta_x, 0, x_blocks - 1)
    source_z = jnp.clip(region_z * z_blocks + block_z + delta_z, 0, N_GZ * z_blocks - 1)
    source_y = jnp.clip(region_y * y_blocks + block_y + delta_y, 0, N_GY * y_blocks - 1)
    region = (source_z // z_blocks) * N_GY + source_y // y_blocks
    inside = (source_x * z_blocks + source_z % z_blocks) * y_blocks + source_y % y_blocks
    return (region * BLK + inside).reshape(-1).astype(jnp.int32)


def reference(volume, shift_code, frac_code, stencil):
    groups = N_GZ * N_GY
    upcoming = jnp.roll(volume, -1, axis=0)

    def forward(items):
        phase_volume, next_phase, codes, code_list = items
        blocks = volume_blocks(phase_volume)
        targets = source_index(codes)
        source = blocks[targets].astype(jnp.float32)
        matrices = block_matrices(code_list.reshape(-1), BS)
        residual = warp_blocks(source, matrices) - volume_blocks(next_phase).astype(jnp.float32)
        residual = block_volume(residual)
        return smooth(jnp.pad(residual, 1), stencil)

    smoothed = lax.map(forward, (volume, upcoming, shift_code, frac_code))

    def backward(items):
        phase_smooth, codes, code_list = items
        targets = source_index(codes)
        matrices = block_matrices(code_list.reshape(-1), BS)
        pulled = adjoint_blocks(volume_blocks(phase_smooth), matrices).reshape(groups * BLK, BS * BS * BS)
        summed = jax.ops.segment_sum(pulled, targets, num_segments=groups * BLK)
        return block_volume(summed.reshape(-1, BS, BS, BS))

    adjoint = lax.map(backward, (smoothed, shift_code, frac_code))
    return adjoint - jnp.roll(smoothed, 1, axis=0)
```

```python
import functools

import jax
import jax.numpy as jnp
from jax import lax
from jax.experimental import pallas as pl
from jax.experimental.pallas import tpu as pltpu
from jax.sharding import PartitionSpec as P

BS = 16
F32 = jnp.float32
BF16 = jnp.bfloat16
I32 = jnp.int32
I16 = jnp.int16
NONE = -4096


def iota(shape, dim, dtype=I32):
    return lax.broadcasted_iota(dtype, shape, dim)


def ring(cells, axis, by):
    count = lax.axis_size(axis)
    return lax.ppermute(cells, axis, [(i, (i + by) % count) for i in range(count)])


def onehot(hit):
    return jnp.where(hit, jnp.array(1, F32), jnp.array(0, F32)).astype(BF16)


def dot(left, right):
    return jnp.dot(left, right, preferred_element_type=F32)


def spread_matrix():
    return onehot(iota((128, 2048), 0) == iota((128, 2048), 1) // BS)


def strip_matrix():
    column = iota((1, 256), 1)
    group = (column % 128) // BS
    wanted = group * 128 + column % BS + (column // 128) * 112
    return onehot(iota((1024, 256), 0) == wanted)


def displacements(codes):
    dx = (codes * 57) >> 9
    rest = codes - 9 * dx
    dz = (rest * 11) >> 5
    dy = rest - 3 * dz
    return dx - 1, dz - 1, dy - 1


def fraction(level):
    return (level + 1).astype(F32) / 5.0


def encode(values, inverse):
    share = values * inverse
    root = share * lax.rsqrt(jnp.abs(share) + 1e-30)
    return jnp.round(root * 32767.0).astype(I32).astype(I16)


def decode(coded, scale):
    count = coded.astype(F32)
    return count * jnp.abs(count) * (scale * (1.0 / (32767.0 * 32767.0)))


def scale_of(message, row):
    return jnp.exp2(message[row : row + 16, :].astype(F32)[2:3])


def pack_kernel(vol, codes, down, up, left, right):
    for p in range(2):
        cells = vol[p]
        rows = pl.ds(p * 1024, 1024)
        down[rows, :] = cells[:, :BS, :].reshape(1024, 128)
        up[rows, :] = cells[:, BS:, :].reshape(1024, 128)
    down[2048:2064, :] = codes[...]
    up[2048:2064, :] = codes[...]
    pack_strips(down, up, left, right)
    left[512:528, :] = codes[...]
    right[512:528, :] = codes[...]


def pack_strips(down, up, left, right):
    chosen = strip_matrix()
    for half, source in enumerate((down, up)):
        wide = jnp.concatenate([source[i * 256 : (i + 1) * 256, :] for i in range(8)], axis=1)
        strips = dot(wide, chosen).astype(BF16)
        left[half * 256 : (half + 1) * 256, :] = strips[:, :128]
        right[half * 256 : (half + 1) * 256, :] = strips[:, 128:]


def corner_kernel(from_left, from_right, down, up):
    for half, out in enumerate((down, up)):
        out[0:256, :] = from_left[half * 256 : (half + 1) * 256, :]
        out[256:512, :] = from_right[half * 256 : (half + 1) * 256, :]
        out[512:528, :] = from_left[512:528, :]
        out[528:544, :] = from_right[512:528, :]


def forward_kernel(
    z_count, y_count, vol, low, high, hleft, hright, clow, chigh, following, codes,
    res, face0, face1, col0, col1, shifts, fracs, keys, weights, mask,
):
    rz = lax.axis_index("gz")
    ry = lax.axis_index("gy")
    spread = dot(codes[...], spread_matrix())
    for i in range(8):
        shifts[i : i + 1, :] = spread[0:1, i * 256 : (i + 1) * 256]
        fracs[i : i + 1, :] = spread[1:2, i * 256 : (i + 1) * 256]
    dx, dz, dy = displacements(shifts[...].astype(I32))
    row = iota((8, 256), 0)
    lane = iota((8, 256), 1)
    bz = lane >> 7
    by = (lane >> 4) & 7
    yy = lane & 15
    bx = row & 3
    source_x = jnp.clip(bx + dx, 0, 3)
    source_z = jnp.clip(rz * 2 + bz + dz, 0, 2 * z_count - 1) - rz * 2 + 1
    source_y = jnp.clip(ry * 8 + by + dy, 0, 8 * y_count - 1) - ry * 8
    inside = (source_y >= 0) & (source_y < 8)
    keys[0] = jnp.where(inside, (source_x - bx + 1) * 4 + source_z, -1)
    keys[1] = source_y * BS + yy
    strip_lane = ((row >> 2) * 4 + source_x) * BS + yy
    keys[2] = jnp.where(source_y < 0, source_z, -1)
    keys[3] = jnp.where(source_y > 7, source_z, -1)
    keys[4] = strip_lane
    levels = fracs[...].astype(I32)
    weights[0] = fraction(levels >> 4)
    weights[1] = fraction((levels >> 2) & 3)
    weights[2] = jnp.where(yy == 15, 0.0, fraction(levels & 3))
    sublane = iota((128, 256), 0)
    last_z = iota((1, BS, 128), 1) == BS - 1
    lanes = iota((BS, 128), 1)

    def step(i, carry):
        p = i // 4
        block = i % 4
        here = [keys[k, pl.ds(i, 1), :] for k in range(5)]
        levels_here = [weights[k, pl.ds(i, 1), :] for k in range(3)]
        pieces = []
        at = 0
        for d in range(3):
            xb = jnp.clip(block + d - 1, 0, 3)
            rows = pl.ds(pl.multiple_of((p * 64 + xb * BS) * BS, 256), 256)
            xs = pl.ds(pl.multiple_of(xb * BS, BS), BS)
            tiles = (
                low[rows, :],
                vol[p, xs, 0:BS, :].reshape(256, 128),
                vol[p, xs, BS : 2 * BS, :].reshape(256, 128),
                high[rows, :],
            )
            for zb in range(4):
                wanted = jnp.where(here[0] == d * 4 + zb, here[1], NONE)
                mask[at : at + 128, :] = onehot(sublane == wanted)
                pieces.append(tiles[zb])
                at += 128
        for side, own, offset in ((2, hleft, 0), (3, hright, 256)):
            tiles = (
                clow[offset : offset + 256, :],
                own[0:256, :],
                own[256:512, :],
                chigh[offset : offset + 256, :],
            )
            for zb in range(4):
                wanted = jnp.where(here[side] == zb, here[4], NONE)
                mask[at : at + 128, :] = onehot(sublane == wanted)
                pieces.append(tiles[zb])
                at += 128
        gathered = dot(jnp.concatenate(pieces, axis=1), mask[...])
        for half in range(2):
            part = slice(half * 128, (half + 1) * 128)
            zs = slice(half * BS, (half + 1) * BS)
            wx, wz, wy = (w[:, part].reshape(1, 1, 128) for w in levels_here)
            wz = jnp.where(last_z, 0.0, wz)
            cells = gathered[:, part].reshape(BS, BS, 128)
            cells = cells + wy * (pltpu.roll(cells, 127, 2) - cells)
            cells = cells + wz * (pltpu.roll(cells, BS - 1, 1) - cells)
            after = jnp.concatenate([cells[1:], cells[BS - 1 :]], axis=0)
            cells = cells + wx * (after - cells)
            xs = pl.ds(pl.multiple_of(block * BS, BS), BS)
            coming = jnp.where(
                p == 0, vol[1, xs, zs, :].astype(F32), following[xs, zs, :].astype(F32)
            )
            cells = cells - coming
            res[p, xs, zs, :] = cells
            out_rows = pl.ds(pl.multiple_of(i * BS, BS), BS)
            if half == 0:
                face0[out_rows, :] = cells[:, 0, :]
            else:
                face1[out_rows, :] = cells[:, BS - 1, :]
            first = col0[zs, :]
            last = col1[zs, :]
            for xi in range(BS):
                at_lane = lanes == i * BS + xi
                first = jnp.where(at_lane, cells[xi, :, 0:1], first)
                last = jnp.where(at_lane, cells[xi, :, 127:128], last)
            col0[zs, :] = first
            col1[zs, :] = last
        return carry

    col0[...] = jnp.zeros((32, 128), F32)
    col1[...] = jnp.zeros((32, 128), F32)
    lax.fori_loop(0, 8, step, 0)


def smooth_kernel(
    z_count, y_count, res, flow, fhigh, cleft, cright, codes, stencil,
    smoothed, down, up, left, right, ahead, low_half, high_half,
):
    rz = lax.axis_index("gz")
    ry = lax.axis_index("gy")
    has_low = (rz > 0).astype(F32)
    has_high = (rz < z_count - 1).astype(F32)
    has_left = (ry > 0).astype(F32)
    has_right = (ry < y_count - 1).astype(F32)
    s0, s1, s2, s3 = (stencil[k] for k in range(4))
    zi = iota((32, 128), 0)
    lane = iota((32, 128), 1)
    edge_left = cleft[...] * has_left
    edge_right = cright[...] * has_right

    def largest(i, peak):
        block = jnp.abs(res[i // 4, pl.ds(pl.multiple_of((i % 4) * BS, BS), BS)])
        return jnp.maximum(peak, jnp.max(block, axis=0))

    peak = jnp.maximum(jnp.abs(edge_left), jnp.abs(edge_right))
    peak = lax.fori_loop(0, 8, largest, peak)
    edge = jnp.maximum(jnp.abs(flow[...]) * has_low, jnp.abs(fhigh[...]) * has_high)
    peak = jnp.maximum(jnp.max(peak), jnp.max(edge)) * (s0 + 2.0 * (s1 + s2 + s3))
    peak = jnp.full((1, 128), jnp.maximum(peak, 1e-30))
    power = jnp.ceil(jnp.log(peak) * 1.4426950408889634)
    inverse = 1.0 / jnp.exp2(power)

    def step(i, carry):
        p = i // 4
        block = i % 4
        x0 = block * BS
        turn = (128 - i * BS) % 128
        lefts = pltpu.roll(edge_left, turn, 1)
        rights = pltpu.roll(edge_right, turn, 1)
        rows = pl.ds(pl.multiple_of(i * BS, BS), BS)
        lows = flow[rows, :] * has_low
        highs = fhigh[rows, :] * has_high
        before = res[p, jnp.maximum(x0 - 1, 0)] * (block > 0).astype(F32)
        cells = res[p, x0]
        for xi in range(BS):
            if xi < BS - 1:
                after = res[p, x0 + xi + 1]
            else:
                after = res[p, jnp.minimum(x0 + BS, 63)] * (block < 3).astype(F32)
            z_low = jnp.where(zi == 0, lows[xi : xi + 1, :], pltpu.roll(cells, 1, 0))
            z_high = jnp.where(zi == 31, highs[xi : xi + 1, :], pltpu.roll(cells, 31, 0))
            y_low = jnp.where(lane == 0, lefts[:, xi : xi + 1], pltpu.roll(cells, 1, 1))
            y_high = jnp.where(lane == 127, rights[:, xi : xi + 1], pltpu.roll(cells, 127, 1))
            value = (
                s0 * cells + s1 * (before + after) + s2 * (z_low + z_high) + s3 * (y_low + y_high)
            )
            smoothed[p, x0 + xi] = value
            rounded = value.astype(BF16)
            coded = encode(value, inverse)
            out_rows = pl.ds(pl.multiple_of((i * BS + xi) * BS, BS), BS)
            low_half[out_rows, :] = rounded[:BS]
            high_half[out_rows, :] = rounded[BS:]
            down[out_rows, :] = coded[:BS]
            up[out_rows, :] = coded[BS:]
            ahead[pl.ds(pl.multiple_of((x0 + xi) * 32, 32), 32), :] = coded
            before = cells
            cells = after
        return carry

    lax.fori_loop(0, 8, step, 0)
    tail = jnp.where(iota((16, 128), 0) == 2, power, codes[...].astype(F32))
    tail = tail.astype(I32).astype(I16)
    down[2048:2064, :] = tail
    up[2048:2064, :] = tail
    ahead[2048:2064, :] = tail
    pack_strips(low_half, high_half, left, right)
    left[512:528, :] = codes[...]
    right[512:528, :] = codes[...]


def turned_warp(cells, wx, wy, wz):
    scaled = wy * cells
    cells = cells - scaled + pltpu.roll(scaled, 1, 2)
    scaled = wz * cells
    cells = cells - scaled + pltpu.roll(scaled, 1, 1)
    scaled = wx * cells[: BS - 1]
    zero = jnp.zeros((1, BS, 128), F32)
    cells = cells - jnp.concatenate([scaled, zero], axis=0) + jnp.concatenate([zero, scaled], axis=0)
    cells = cells.reshape(256, 128)
    high = cells.astype(BF16)
    return high, (cells - high.astype(F32)).astype(BF16)


def adjoint_kernel(
    z_count, y_count, smoothed, low, high, hleft, hright, clow, chigh, earlier, codes,
    out, shifts, fracs, weights, turned, pulled, mask,
):
    rz = lax.axis_index("gz")
    ry = lax.axis_index("gy")
    spread = spread_matrix()
    own = dot(codes[...], spread)
    below = dot(low[2048:2064, :].astype(F32).astype(BF16), spread)
    above = dot(high[2048:2064, :].astype(F32).astype(BF16), spread)
    low_scale = scale_of(low, 2048)
    high_scale = scale_of(high, 2048)
    earlier_scale = scale_of(earlier, 2048)
    for i in range(8):
        for zb, (source, half) in enumerate(((below, 1), (own, 0), (own, 1), (above, 0))):
            part = slice(i * 256 + half * 128, i * 256 + half * 128 + 128)
            shifts[i * 4 + zb : i * 4 + zb + 1, :] = source[0:1, part]
            fracs[i * 4 + zb : i * 4 + zb + 1, :] = source[1:2, part]
    column = iota((128, 128), 1)
    for side, (own_strip, offset, edge) in enumerate(((hleft, 512, 7), (hright, 528, 0))):
        for zb, (source, first, half) in enumerate(
            ((clow, offset, 1), (own_strip, 512, 0), (own_strip, 512, 1), (chigh, offset, 0))
        ):
            block = (column >> 6) * 64 + (((column >> 4) & 3) * 2 + half) * 8 + edge
            picked = dot(source[first : first + 16, :], onehot(iota((128, 128), 0) == block))
            at = 32 + side * 4 + zb
            shifts[at : at + 1, :] = picked[0:1, :]
            fracs[at : at + 1, :] = picked[1:2, :]
    dx, dz, dy = displacements(shifts[...].astype(I32))
    row = iota((40, 128), 0)
    lane = iota((40, 128), 1)
    strip = row >= 32
    zb = row & 3
    yy = lane & 15
    number = jnp.where(strip, lane >> 4, row >> 2)
    bx = number & 3
    by = jnp.where(strip, jnp.where(row < 36, -1, 8), lane >> 4)
    dest_z = rz * 2 + zb - 1
    dest_y = ry * 8 + by
    there = (dest_z >= 0) & (dest_z < 2 * z_count) & (dest_y >= 0) & (dest_y < 8 * y_count)
    source_x = jnp.clip(bx + dx, 0, 3)
    source_z = jnp.clip(dest_z + dz, 0, 2 * z_count - 1) - rz * 2
    source_y = jnp.clip(dest_y + dy, 0, 8 * y_count - 1) - ry * 8
    there = there & (source_z >= 0) & (source_z < 2) & (source_y >= 0) & (source_y < 8)
    target = ((number >> 2) * 4 + source_x) * 256 + source_z * 128 + source_y * BS + yy
    target = jnp.where(there, target, NONE).astype(F32)
    nobody = jnp.full((32, 128), float(NONE), F32)
    target = jnp.concatenate([target[:32], nobody, target[32:], nobody, nobody[:24]], axis=0)
    turned[...] = target.T
    levels = fracs[...].astype(I32)
    weights[0] = fraction(levels >> 4)
    weights[1] = fraction((levels >> 2) & 3)
    weights[2] = jnp.where(yy == 15, 0.0, fraction(levels & 3))
    last_z = iota((1, BS, 128), 1) == BS - 1

    def weights_of(r):
        wx, wz, wy = (weights[k, pl.ds(r, 1), :].reshape(1, 1, 128) for k in range(3))
        return wx, wy, jnp.where(last_z, 0.0, wz)

    def pull(i, carry):
        p = i // 4
        xs = pl.ds(pl.multiple_of((i % 4) * BS, BS), BS)
        rows = pl.ds(pl.multiple_of(i * 256, 256), 256)
        tiles = (
            decode(low[rows, :], low_scale).reshape(BS, BS, 128),
            smoothed[p, xs, 0:BS, :],
            smoothed[p, xs, BS : 2 * BS, :],
            decode(high[rows, :], high_scale).reshape(BS, BS, 128),
        )
        for zb in range(4):
            first, second = turned_warp(tiles[zb], *weights_of(i * 4 + zb))
            pulled[i * 4 + zb, 0:256, :] = first
            pulled[i * 4 + zb, 256:512, :] = second
        return carry

    lax.fori_loop(0, 8, pull, 0)
    for side, (own_strip, offset) in enumerate(((hleft, 0), (hright, 256))):
        tiles = (
            clow[offset : offset + 256, :],
            own_strip[0:256, :],
            own_strip[256:512, :],
            chigh[offset : offset + 256, :],
        )
        for zb in range(4):
            at = 32 + side * 4 + zb
            cells = tiles[zb].astype(F32).reshape(BS, BS, 128)
            first, second = turned_warp(cells, *weights_of(at))
            pulled[at, 0:256, :] = first
            pulled[at, 256:512, :] = second

    lanes = iota((128, 256), 1)

    def step(i, carry):
        p = i // 4
        wanted = (lanes + i * 256).astype(F32)
        near = pltpu.roll(turned[...], (132 - i * 4) % 128, 1)
        pieces = []
        at = 0
        for d in range(3):
            number = jnp.clip(i + d - 1, 0, 7)
            for zb in range(4):
                column = near[:, d * 4 + zb : d * 4 + zb + 1]
                mask[at : at + 128, :] = onehot(column == wanted)
                pieces.append(pulled[number * 4 + zb])
                at += 128
        for r in range(32, 40):
            mask[at : at + 128, :] = onehot(turned[:, r + 32 : r + 33] == wanted)
            pieces.append(pulled[r])
            at += 128
        both = dot(jnp.concatenate(pieces, axis=1), mask[...])
        total = both[0:256] + both[256:512]
        xs = pl.ds(pl.multiple_of((i % 4) * BS, BS), BS)
        rows = pl.ds(pl.multiple_of((i % 4) * 512, 512), 512)
        passed = decode(earlier[rows, :], earlier_scale).reshape(BS, 2 * BS, 128)
        for half in range(2):
            zs = slice(half * BS, (half + 1) * BS)
            cells = total[:, half * 128 : (half + 1) * 128].reshape(BS, BS, 128)
            before = jnp.where(p == 0, passed[:, zs], smoothed[0, xs, zs, :])
            out[p, xs, zs, :] = cells - before
        return carry

    lax.fori_loop(0, 8, step, 0)


PARAMS = pltpu.CompilerParams(vmem_limit_bytes=50 * 1024 * 1024)


def shape(dims, dtype):
    return jax.ShapeDtypeStruct(dims, dtype)


def halo(down, up, left, right):
    high = ring(down, "gz", -1)
    low = ring(up, "gz", 1)
    hright = ring(left, "gy", -1)
    hleft = ring(right, "gy", 1)
    corner = shape((544, 128), BF16)
    corner_down, corner_up = pl.pallas_call(corner_kernel, out_shape=(corner, corner))(hleft, hright)
    chigh = ring(corner_down, "gz", -1)
    clow = ring(corner_up, "gz", 1)
    return low, high, hleft, hright, clow, chigh


def body(volume, shift_code, frac_code, stencil):
    z_count = lax.axis_size("gz")
    y_count = lax.axis_size("gy")
    codes = jnp.concatenate(
        [shift_code.reshape(1, 128), frac_code.reshape(1, 128), jnp.zeros((14, 128), I32)]
    ).astype(BF16)
    slab = shape((2064, 128), BF16)
    coded = shape((2064, 128), I16)
    strip = shape((528, 128), BF16)
    packed = pl.pallas_call(
        pack_kernel, out_shape=(slab, slab, strip, strip), compiler_params=PARAMS
    )(volume, codes)
    following = ring(volume[0], "phase", -1)
    near = halo(*packed)
    face = shape((128, 128), F32)
    column = shape((32, 128), F32)
    res, face0, face1, col0, col1 = pl.pallas_call(
        functools.partial(forward_kernel, z_count, y_count),
        out_shape=(shape(volume.shape, F32), face, face, column, column),
        scratch_shapes=[
            pltpu.VMEM((8, 256), F32),
            pltpu.VMEM((8, 256), F32),
            pltpu.VMEM((5, 8, 256), I32),
            pltpu.VMEM((3, 8, 256), F32),
            pltpu.VMEM((2560, 256), BF16),
        ],
        compiler_params=PARAMS,
    )(volume, *near, following, codes)
    fhigh = ring(face0, "gz", -1)
    flow = ring(face1, "gz", 1)
    cright = ring(col0, "gy", -1)
    cleft = ring(col1, "gy", 1)
    vmem = pl.BlockSpec(memory_space=pltpu.VMEM)
    smoothed, down, up, left, right, ahead = pl.pallas_call(
        functools.partial(smooth_kernel, z_count, y_count),
        out_shape=(
            shape(volume.shape, F32), coded, coded, strip, strip, coded,
        ),
        scratch_shapes=[pltpu.VMEM((2048, 128), BF16), pltpu.VMEM((2048, 128), BF16)],
        in_specs=[vmem] * 6 + [pl.BlockSpec(memory_space=pltpu.SMEM)],
        compiler_params=PARAMS,
    )(res, flow, fhigh, cleft, cright, codes, stencil)
    near = halo(down, up, left, right)
    earlier = ring(ahead, "phase", 1)
    return pl.pallas_call(
        functools.partial(adjoint_kernel, z_count, y_count),
        out_shape=shape(volume.shape, F32),
        scratch_shapes=[
            pltpu.VMEM((40, 128), F32),
            pltpu.VMEM((40, 128), F32),
            pltpu.VMEM((3, 40, 128), F32),
            pltpu.VMEM((128, 128), F32),
            pltpu.VMEM((40, 512, 128), BF16),
            pltpu.VMEM((2560, 256), BF16),
        ],
        compiler_params=PARAMS,
    )(smoothed, *near, earlier, codes)


def solution(mesh):
    placed = (
        P("phase", None, "gz", "gy"),
        P("phase", "gz", "gy", None),
        P("phase", "gz", "gy", None),
        P(),
    )
    return jax.shard_map(
        body, mesh=mesh, in_specs=placed, out_specs=P("phase", None, "gz", "gy"), check_vma=False
    )
```

```python
import functools

import jax
import jax.numpy as jnp
from jax import lax
from jax.experimental import pallas as pl
from jax.experimental.pallas import tpu as pltpu
from jax.sharding import PartitionSpec as P

BS = 16
F32 = jnp.float32
BF16 = jnp.bfloat16
I32 = jnp.int32
I16 = jnp.int16
NONE = -4096


def iota(shape, dim, dtype=I32):
    return lax.broadcasted_iota(dtype, shape, dim)


def ring(cells, axis, by):
    count = lax.axis_size(axis)
    return lax.ppermute(cells, axis, [(i, (i + by) % count) for i in range(count)])


def onehot(hit):
    return jnp.where(hit, jnp.array(1, BF16), jnp.array(0, BF16))


def dot(left, right):
    return jnp.dot(left, right, preferred_element_type=F32)


def spread_matrix():
    return onehot(iota((128, 2048), 0, I16) == (iota((1, 2048), 1) >> 4).astype(I16))


def strip_matrix():
    column = iota((1, 256), 1)
    group = (column % 128) // BS
    wanted = group * 128 + column % BS + (column // 128) * 112
    return onehot(iota((1024, 256), 0, I16) == wanted.astype(I16))


def displacements(codes):
    dx = (codes * 57) >> 9
    rest = codes - 9 * dx
    dz = (rest * 11) >> 5
    dy = rest - 3 * dz
    return dx - 1, dz - 1, dy - 1


def fraction(level):
    return (level + 1).astype(F32) / 5.0


def encode(values, inverse):
    share = values * inverse
    root = share * lax.rsqrt(jnp.abs(share) + 1e-30)
    return jnp.round(root * 32767.0).astype(I32).astype(I16)


def decode(coded, scale):
    count = coded.astype(F32)
    return count * jnp.abs(count) * (scale * (1.0 / (32767.0 * 32767.0)))


def scale_of(message, row):
    return jnp.exp2(message[row : row + 16, :].astype(F32)[2:3])


def pack_kernel(vol, shift, frac, left, right, first, codes):
    rows = [
        jnp.concatenate([part[0, 0].astype(F32), part[1, 0].astype(F32)], axis=1)
        for part in (shift, frac)
    ]
    at = iota((BS, 128), 0)
    codes[...] = jnp.where(at == 0, rows[0], jnp.where(at == 1, rows[1], 0.0)).astype(BF16)
    first[...] = vol[0]
    tiles = [
        [
            vol[i // 4, (i % 4) * BS : (i % 4 + 1) * BS, h * BS : (h + 1) * BS].reshape(256, 128)
            for i in range(8)
        ]
        for h in range(2)
    ]
    for h, strips in enumerate(pack_strips(tiles)):
        left[h * 256 : (h + 1) * 256, :] = strips[:, :128]
        right[h * 256 : (h + 1) * 256, :] = strips[:, 128:]


def pack_strips(tiles):
    chosen = strip_matrix()
    return [dot(jnp.concatenate(half, axis=1), chosen).astype(BF16) for half in tiles]


def slab_kernel(vol, hleft, hright, down, up):
    for half, out in enumerate((down, up)):
        for p in range(2):
            cells = vol[p, :, half * BS : (half + 1) * BS, :]
            out[p * 1024 : (p + 1) * 1024, :] = cells.reshape(1024, 128)
        for side, strip in enumerate((hleft, hright)):
            at = 2048 + side * 256
            out[at : at + 256, :] = strip[half * 256 : (half + 1) * 256, :]


def near_kernel(
    z_count, y_count, vol, hleft, hright, codes,
    gathered, keys, weights, shifts, fracs, mask,
):
    rz = lax.axis_index("gz")
    ry = lax.axis_index("gy")
    spread = dot(codes[...], spread_matrix())
    for i in range(8):
        shifts[i : i + 1, :] = spread[0:1, i * 256 : (i + 1) * 256]
        fracs[i : i + 1, :] = spread[1:2, i * 256 : (i + 1) * 256]
    dx, dz, dy = displacements(shifts[...].astype(I32))
    row = iota((8, 256), 0)
    lane = iota((8, 256), 1)
    bz = lane >> 7
    by = (lane >> 4) & 7
    yy = lane & 15
    bx = row & 3
    source_x = jnp.clip(bx + dx, 0, 3)
    source_z = jnp.clip(rz * 2 + bz + dz, 0, 2 * z_count - 1) - rz * 2 + 1
    source_y = jnp.clip(ry * 8 + by + dy, 0, 8 * y_count - 1) - ry * 8
    inside = (source_y >= 0) & (source_y < 8)
    keys[0] = jnp.where(inside, (source_x - bx + 1) * 4 + source_z, -1)
    keys[1] = source_y * BS + yy
    strip_lane = ((row >> 2) * 4 + source_x) * BS + yy
    keys[2] = jnp.where(source_y < 0, source_z, -1)
    keys[3] = jnp.where(source_y > 7, source_z, -1)
    keys[4] = strip_lane
    levels = fracs[...].astype(I32)
    weights[0] = fraction(levels >> 4)
    weights[1] = fraction((levels >> 2) & 3)
    weights[2] = jnp.where(yy == 15, 0.0, fraction(levels & 3))

    def step(block, carry):
        for p in range(2):

            def tile(xb, zb):
                xs = pl.ds(pl.multiple_of(xb * BS, BS), BS)
                return vol[p, xs, (zb - 1) * BS : zb * BS, :].reshape(256, 128)

            strips = [[half[0:256, :], half[256:512, :]] for half in (hleft, hright)]
            i = p * 4 + block
            gathered[i] = gather(i, keys, mask.at[p], tile, strips, (1, 2))
        return carry

    lax.fori_loop(0, 4, step, 0)


def gather(i, keys, mask, tile, strips, z_blocks):
    here = [keys[k, pl.ds(i, 1), :] for k in range(5)]
    sublane = iota((128, 256), 0, I16)
    pieces = []

    def add(piece, hit, place):
        at = len(pieces) * 128
        mask[at : at + 128, :] = onehot(sublane == jnp.where(hit, place, NONE).astype(I16))
        pieces.append(piece)

    for d in range(3):
        xb = jnp.clip(i % 4 + d - 1, 0, 3)
        for zb in z_blocks:
            add(tile(xb, zb), here[0] == d * 4 + zb, here[1])
    for side in range(2):
        for k, zb in enumerate(z_blocks):
            add(strips[side][k], here[2 + side] == zb, here[4])
    return dot(jnp.concatenate(pieces, axis=1), mask[...])


def forward_kernel(
    vol, low, high, following, partial, keys, weights, codes, stencil,
    smoothed, left, right, face0, face1, res_left, res_right, peak,
    mask, res, strips_in,
):
    s0, s1, s2, s3 = (stencil[k] for k in range(4))
    last_z = iota((1, BS, 128), 1) == BS - 1

    def step(block, carry):
        xs = pl.ds(pl.multiple_of(block * BS, BS), BS)
        for p in range(2):
            i = p * 4 + block

            def tile(xb, zb):
                rows = pl.ds(pl.multiple_of((p * 64 + xb * BS) * BS, 256), 256)
                return (low if zb == 0 else high)[rows, :]

            strips = [
                [slab[2048 + k * 256 : 2304 + k * 256, :] for slab in (low, high)] for k in range(2)
            ]
            gathered = partial[i] + gather(i, keys, mask.at[p], tile, strips, (0, 3))
            levels_here = [weights[k, pl.ds(i, 1), :] for k in range(3)]
            for half in range(2):
                part = slice(half * 128, (half + 1) * 128)
                zs = slice(half * BS, (half + 1) * BS)
                wx, wz, wy = (w[:, part].reshape(1, 1, 128) for w in levels_here)
                wz = jnp.where(last_z, 0.0, wz)
                cells = gathered[:, part].reshape(BS, BS, 128)
                cells = cells + wy * (pltpu.roll(cells, 127, 2) - cells)
                cells = cells + wz * (pltpu.roll(cells, BS - 1, 1) - cells)
                after = jnp.concatenate([cells[1:], cells[BS - 1 :]], axis=0)
                cells = cells + wx * (after - cells)
                coming = vol[1, xs, zs, :] if p == 0 else following[xs, zs, :]
                cells = cells - coming.astype(F32)
                res[p, xs, zs, :] = cells
                rounded = cells.astype(BF16)
                strips_in[half, i] = rounded.reshape(256, 128)
                out_rows = pl.ds(pl.multiple_of(i * BS, BS), BS)
                if half == 0:
                    face0[out_rows, :] = cells[:, 0, :].astype(BF16)
                else:
                    face1[out_rows, :] = cells[:, BS - 1, :].astype(BF16)
        return carry

    lax.fori_loop(0, 4, step, 0)
    packed = pack_strips([[strips_in[half, i] for i in range(8)] for half in range(2)])
    for half in range(2):
        rows = slice(half * 256, (half + 1) * 256)
        res_left[rows, :] = packed[half][:, :128]
        res_right[rows, :] = packed[half][:, 128:]
    group = iota((BS, 128), 1) & 15
    for out, side, edge in ((left, 0, 0), (right, 1, 15)):
        out[512:528, :] = codes[...]
        for half in range(2):
            cells = packed[half][:, side * 128 : (side + 1) * 128].astype(F32).reshape(BS, BS, 128)
            column = jnp.zeros((BS, 128), F32)
            for xi in range(BS):
                turn = (xi - edge) % 128
                plane = pltpu.roll(cells[xi], turn, 1) if turn else cells[xi]
                column = jnp.where(group == xi, plane, column)
            out[528 + half * BS : 544 + half * BS, :] = column.astype(BF16)
            rows = slice(560 + half * BS, 576 + half * BS)
            out[rows, :] = cells[:, half * (BS - 1), :].astype(BF16)

    zi = iota((32, 128), 0)
    lane = iota((32, 128), 1)

    def smooth(block, tops):
        x0 = block * BS
        out = []
        for p in range(2):
            top = tops[p]
            before = res[p, jnp.maximum(x0 - 1, 0)] * (block > 0).astype(F32)
            cells = res[p, x0]
            for xi in range(BS):
                if xi < BS - 1:
                    after = res[p, x0 + xi + 1]
                else:
                    after = res[p, jnp.minimum(x0 + BS, 63)] * (block < 3).astype(F32)
                top = jnp.maximum(top, jnp.abs(cells))
                z_low = jnp.where(zi == 0, 0.0, pltpu.roll(cells, 1, 0))
                z_high = jnp.where(zi == 31, 0.0, pltpu.roll(cells, 31, 0))
                y_low = jnp.where(lane == 0, 0.0, pltpu.roll(cells, 1, 1))
                y_high = jnp.where(lane == 127, 0.0, pltpu.roll(cells, 127, 1))
                value = s0 * cells + s1 * (before + after)
                value = value + s2 * (z_low + z_high) + s3 * (y_low + y_high)
                smoothed[p, x0 + xi] = value
                rounded = value.astype(BF16)
                rows = pl.ds(xi * BS, BS)
                strips_in[0, p * 4 + block, rows, :] = rounded[:BS]
                strips_in[1, p * 4 + block, rows, :] = rounded[BS:]
                before = cells
                cells = after
            out.append(top)
        return tuple(out)

    zero = jnp.zeros((32, 128), F32)
    tops = lax.fori_loop(0, 4, smooth, (zero, zero))
    peak[...] = jnp.maximum(tops[0], tops[1])
    packed = pack_strips([[strips_in[half, i] for i in range(8)] for half in range(2)])
    for half in range(2):
        rows = slice(half * 256, (half + 1) * 256)
        left[rows, :] = packed[half][:, :128]
        right[rows, :] = packed[half][:, 128:]


def complete_kernel(
    z_count, y_count, partial, flow, fhigh, hleft, hright, res_left, res_right, peak, codes, stencil,
    smoothed, down, up, ahead, left, right,
):
    rz = lax.axis_index("gz")
    ry = lax.axis_index("gy")
    has_low = (rz > 0).astype(F32)
    has_high = (rz < z_count - 1).astype(F32)
    s0, s1, s2, s3 = (stencil[k] for k in range(4))
    columns = [
        hleft[528:560, :].astype(F32) * (ry > 0).astype(F32),
        hright[528:560, :].astype(F32) * (ry < y_count - 1).astype(F32),
    ]
    flows = flow[...].astype(F32) * has_low
    fhighs = fhigh[...].astype(F32) * has_high
    group = iota((256, 128), 1) & 15
    strips = []
    for out, theirs, own, edge in ((left, hleft, res_left, 15), (right, hright, res_right, 0)):
        for half in range(2):
            rows = slice(half * 256, (half + 1) * 256)
            beside = pltpu.roll(own[rows, :].astype(F32), 15 if edge else 113, 1)
            cells = theirs[rows, :].astype(F32) + jnp.where(group == edge, s3 * beside, 0.0)
            out[rows, :] = cells.astype(BF16)
            strips.append(cells)

    inner = jnp.max(peak[...])
    for cells in (flows, fhighs, *columns):
        inner = jnp.maximum(inner, jnp.max(jnp.abs(cells)))
    top = inner * (s0 + 2.0 * (s1 + s2 + s3))
    edges = [part[560:592, :].astype(F32) for part in (hleft, hright)]
    for cells in (*strips, *edges):
        top = jnp.maximum(top, jnp.max(jnp.abs(cells)))
    top = jnp.full((1, 128), jnp.maximum(top, 1e-30))
    power = jnp.ceil(jnp.log(top) * 1.4426950408889634)
    inverse = 1.0 / jnp.exp2(power)
    for half, out in enumerate((down, up)):
        for side in range(2):
            at = 2048 + side * 256
            out[at : at + 256, :] = encode(strips[side * 2 + half], inverse)
            at = 2560 + side * BS
            out[at : at + BS, :] = encode(edges[side][half * BS : (half + 1) * BS], inverse)
        tail = jnp.where(iota((BS, 128), 0) == 2, power, codes[...].astype(F32))
        tails = [tail] + [part[512:528, :].astype(F32) for part in (hleft, hright)]
        for k, tail in enumerate(tails):
            out[2592 + k * BS : 2608 + k * BS, :] = tail.astype(I32).astype(I16)
        if half == 0:
            ahead[2048:2064, :] = tails[0].astype(I32).astype(I16)

    lane = iota((32, 128), 1)
    turned = pltpu.roll(columns[1], 127, 1)
    parity = [
        jnp.where((lane & 1) == odd, columns[0], turned) for odd in range(2)
    ]
    at_edge = (lane == 0) | (lane == 127)
    zi = iota((32, 128), 0)
    low_edge = zi == 0
    high_edge = zi == 31

    def step(block, carry):
        for p in range(2):
            i = p * 4 + block
            turn = (128 - i * BS) % 128
            sides = [pltpu.roll(part, turn, 1) for part in parity]
            rows = pl.ds(pl.multiple_of(i * BS, BS), BS)
            lows = flow[rows, :].astype(F32) * (s2 * has_low)
            highs = fhigh[rows, :].astype(F32) * (s2 * has_high)
            for xi in range(BS):
                side = sides[xi & 1]
                if xi:
                    side = pltpu.roll(side, 128 - xi, 1)
                x = block * BS + xi
                value = partial[p, x] + jnp.where(at_edge, s3 * side, 0.0)
                value = value + jnp.where(low_edge, lows[xi : xi + 1], 0.0)
                value = value + jnp.where(high_edge, highs[xi : xi + 1], 0.0)
                smoothed[p, x] = value
                coded = encode(value, inverse)
                out_rows = pl.ds(pl.multiple_of((i * BS + xi) * BS, BS), BS)
                down[out_rows, :] = coded[:BS]
                up[out_rows, :] = coded[BS:]
                if p == 1:
                    ahead[pl.ds(pl.multiple_of(x * 32, 32), 32), :] = coded
        return carry

    lax.fori_loop(0, 4, step, 0)


def turned_warp(cells, wx, wy, wz):
    scaled = wy * cells
    cells = cells - scaled + pltpu.roll(scaled, 1, 2)
    scaled = wz * cells
    cells = cells - scaled + pltpu.roll(scaled, 1, 1)
    scaled = wx * cells[: BS - 1]
    zero = jnp.zeros((1, BS, 128), F32)
    cells = cells - jnp.concatenate([scaled, zero], axis=0) + jnp.concatenate([zero, scaled], axis=0)
    cells = cells.reshape(256, 128)
    high = cells.astype(BF16)
    return high, (cells - high.astype(F32)).astype(BF16)


def targets(z_count, y_count, shifts, fracs, z_blocks, turned, weights):
    pair, along = z_blocks
    rz = lax.axis_index("gz")
    ry = lax.axis_index("gy")
    dx, dz, dy = displacements(shifts[...].astype(I32))
    row = iota((24, 128), 0)
    lane = iota((24, 128), 1)
    strip = row >= 16
    zb = jnp.where(strip, row & 3, jnp.where((row & 1) == 0, pair[0], pair[1]))
    yy = lane & 15
    number = jnp.where(strip, lane >> 4, row >> 1)
    bx = number & 3
    by = jnp.where(strip, jnp.where(row < 20, -1, 8), lane >> 4)
    dest_z = rz * 2 + zb - 1
    dest_y = ry * 8 + by
    there = (dest_z >= 0) & (dest_z < 2 * z_count) & (dest_y >= 0) & (dest_y < 8 * y_count)
    source_x = jnp.clip(bx + dx, 0, 3)
    source_z = jnp.clip(dest_z + dz, 0, 2 * z_count - 1) - rz * 2
    source_y = jnp.clip(dest_y + dy, 0, 8 * y_count - 1) - ry * 8
    there = there & (source_z >= 0) & (source_z < 2) & (source_y >= 0) & (source_y < 8)
    target = ((number >> 2) * 4 + source_x) * 256 + source_z * 128 + source_y * BS + yy
    target = jnp.where(there, target, NONE).astype(F32)
    nobody = jnp.full((104, 128), float(NONE), F32)
    columns = jnp.concatenate([target, nobody], axis=0).T
    for r in range(16 + 2 * len(along)):
        turned[r] = jnp.broadcast_to(columns[:, r : r + 1], (128, 128)).astype(I16)
    levels = fracs[...].astype(I32)
    weights[0] = fraction(levels >> 4)
    weights[1] = fraction((levels >> 2) & 3)
    weights[2] = jnp.where(yy == 15, 0.0, fraction(levels & 3))


def strip_codes(at, source, half, edge, shifts, fracs):
    column = iota((1, 128), 1)
    block = (column >> 6) * 64 + (((column >> 4) & 3) * 2 + half) * 8 + edge
    picked = dot(source, onehot(iota((128, 128), 0, I16) == block.astype(I16)))
    shifts[at : at + 1, :] = picked[0:1, :]
    fracs[at : at + 1, :] = picked[1:2, :]


def pull_all(tiles_of, strips, weights, pulled):
    last_z = iota((1, BS, 128), 1) == BS - 1

    def put(r, cells):
        wx, wz, wy = (weights[k, pl.ds(r, 1), :].reshape(1, 1, 128) for k in range(3))
        first, second = turned_warp(cells, wx, wy, jnp.where(last_z, 0.0, wz))
        pulled[r, 0:256, :] = first
        pulled[r, 256:512, :] = second

    def pull(i, carry):
        for k, cells in enumerate(tiles_of(i)):
            put(i * 2 + k, cells)
        return carry

    lax.fori_loop(0, 8, pull, 0)
    for k, cells in enumerate(strips):
        put(16 + k, cells)


def collect(i, turned, pulled, mask, strips):
    lanes = iota((128, 256), 1, I16) + (i * 256).astype(I16)
    pieces = []

    def add(r, hit):
        at = len(pieces) * 128
        column = turned[r]
        column = jnp.concatenate([column, column], axis=1)
        if hit is not None:
            column = jnp.where(hit, column, jnp.full_like(column, NONE))
        mask[at : at + 128, :] = onehot(column == lanes)
        pieces.append(pulled[r])

    for d in range(3):
        number = jnp.clip(i + d - 1, 0, 7)
        hit = None if d == 1 else number != i
        for k in range(2):
            add(number * 2 + k, hit)
    for r in range(16, 16 + strips):
        add(r, None)
    both = dot(jnp.concatenate(pieces, axis=1), mask[...])
    return both[0:256] + both[256:512]


def inner_kernel(
    z_count, y_count, smoothed, codes,
    out, shifts, fracs, weights, turned, pulled, mask,
):
    own = dot(codes[...], spread_matrix())
    shifts[...] = jnp.zeros((24, 128), F32)
    fracs[...] = jnp.zeros((24, 128), F32)
    for i in range(8):
        for half in range(2):
            part = slice(i * 256 + half * 128, i * 256 + half * 128 + 128)
            shifts[i * 2 + half : i * 2 + half + 1, :] = own[0:1, part]
            fracs[i * 2 + half : i * 2 + half + 1, :] = own[1:2, part]
    targets(z_count, y_count, shifts, fracs, ((1, 2), ()), turned, weights)

    def tiles_of(i):
        xs = pl.ds(pl.multiple_of((i % 4) * BS, BS), BS)
        return smoothed[i // 4, xs, 0:BS, :], smoothed[i // 4, xs, BS : 2 * BS, :]

    pull_all(tiles_of, (), weights, pulled)

    def step(block, carry):
        xs = pl.ds(pl.multiple_of(block * BS, BS), BS)
        for p in range(2):
            total = collect(p * 4 + block, turned, pulled, mask.at[p], 0)
            for half in range(2):
                zs = slice(half * BS, (half + 1) * BS)
                cells = total[:, half * 128 : (half + 1) * 128].reshape(BS, BS, 128)
                out[p, xs, zs, :] = cells if p == 0 else cells - smoothed[0, xs, zs, :]
        return carry

    lax.fori_loop(0, 4, step, 0)


def outer_kernel(
    z_count, y_count, partial, low, high, hleft, hright, left, right, earlier, stencil,
    out, shifts, fracs, weights, turned, pulled, mask,
):
    rz = lax.axis_index("gz")
    s2 = stencil[2]
    has_low = (rz > 0).astype(F32) * s2
    has_high = (rz < z_count - 1).astype(F32) * s2
    shifts[...] = jnp.zeros((24, 128), F32)
    fracs[...] = jnp.zeros((24, 128), F32)
    spread = spread_matrix()
    tails = [
        [slab[2592 + k * BS : 2608 + k * BS, :].astype(F32).astype(BF16) for k in range(3)]
        for slab in (low, high)
    ]
    for k, half in ((0, 1), (1, 0)):
        theirs = dot(tails[k][0], spread)
        for i in range(8):
            part = slice(i * 256 + half * 128, i * 256 + half * 128 + 128)
            shifts[i * 2 + k : i * 2 + k + 1, :] = theirs[0:1, part]
            fracs[i * 2 + k : i * 2 + k + 1, :] = theirs[1:2, part]
    for side, (strip, edge) in enumerate(((hleft, 7), (hright, 0))):
        at = 16 + side * 4
        beside = strip[512:528, :]
        strip_codes(at, tails[0][1 + side], 1, edge, shifts, fracs)
        strip_codes(at + 1, beside, 0, edge, shifts, fracs)
        strip_codes(at + 2, beside, 1, edge, shifts, fracs)
        strip_codes(at + 3, tails[1][1 + side], 0, edge, shifts, fracs)
    targets(z_count, y_count, shifts, fracs, ((0, 3), (0, 1, 2, 3)), turned, weights)
    low_scale = scale_of(low, 2592)
    high_scale = scale_of(high, 2592)
    earlier_scale = scale_of(earlier, 2048)
    zi = iota((1, BS, 128), 1)

    def with_row(cells, row, values):
        return cells + jnp.where(zi == row, values.reshape(BS, 1, 128), 0.0)

    def tiles_of(i):
        rows = pl.ds(pl.multiple_of(i * 256, 256), 256)
        return (
            decode(low[rows, :], low_scale).reshape(BS, BS, 128),
            decode(high[rows, :], high_scale).reshape(BS, BS, 128),
        )

    strips = []
    for side, (strip, own) in enumerate(((hleft, left), (hright, right))):
        corner = slice(2048 + side * 256, 2304 + side * 256)
        edge = slice(2560 + side * BS, 2576 + side * BS)
        below = decode(low[corner, :], low_scale).reshape(BS, BS, 128)
        above = decode(high[corner, :], high_scale).reshape(BS, BS, 128)
        first = own[0:256, :].astype(F32).reshape(BS, BS, 128)
        second = own[256:512, :].astype(F32).reshape(BS, BS, 128)
        strips += [
            with_row(below, BS - 1, s2 * strip[560:576, :].astype(F32)),
            with_row(first, 0, has_low * decode(low[edge, :], low_scale)),
            with_row(second, BS - 1, has_high * decode(high[edge, :], high_scale)),
            with_row(above, 0, s2 * strip[576:592, :].astype(F32)),
        ]
    pull_all(tiles_of, strips, weights, pulled)

    def step(block, carry):
        xs = pl.ds(pl.multiple_of(block * BS, BS), BS)
        rows = pl.ds(pl.multiple_of(block * 512, 512), 512)
        for p in range(2):
            total = collect(p * 4 + block, turned, pulled, mask.at[p], 8)
            for half in range(2):
                zs = slice(half * BS, (half + 1) * BS)
                cells = total[:, half * 128 : (half + 1) * 128].reshape(BS, BS, 128)
                cells = cells + partial[p, xs, zs, :]
                if p == 0:
                    passed = decode(earlier[rows, :], earlier_scale).reshape(BS, 2 * BS, 128)
                    cells = cells - passed[:, zs]
                out[p, xs, zs, :] = cells
        return carry

    lax.fori_loop(0, 4, step, 0)


PARAMS = pltpu.CompilerParams(vmem_limit_bytes=50 * 1024 * 1024)


def shape(dims, dtype):
    return jax.ShapeDtypeStruct(dims, dtype)


def body(volume, shift_code, frac_code, stencil):
    z_count = lax.axis_size("gz")
    y_count = lax.axis_size("gy")
    strip = shape((512, 128), BF16)
    grid = shape(volume.shape, F32)
    plane = shape((128, 128), BF16)
    vmem = pl.BlockSpec(memory_space=pltpu.VMEM)
    smem = pl.BlockSpec(memory_space=pltpu.SMEM)
    left, right, first, codes = pl.pallas_call(
        pack_kernel,
        out_shape=(strip, strip, shape(volume.shape[1:], BF16), shape((BS, 128), BF16)),
        compiler_params=PARAMS,
    )(volume, shift_code, frac_code)
    hright = ring(left, "gy", -1)
    hleft = ring(right, "gy", 1)
    following = ring(first, "phase", -1)
    slab = shape((2560, 128), BF16)
    down, up = pl.pallas_call(slab_kernel, out_shape=(slab, slab), compiler_params=PARAMS)(
        volume, hleft, hright
    )
    high = ring(down, "gz", -1)
    low = ring(up, "gz", 1)
    partial, keys, weights = pl.pallas_call(
        functools.partial(near_kernel, z_count, y_count),
        out_shape=(shape((8, 256, 256), F32), shape((5, 8, 256), I32), shape((3, 8, 256), F32)),
        scratch_shapes=[
            pltpu.VMEM((8, 256), F32),
            pltpu.VMEM((8, 256), F32),
            pltpu.VMEM((2, 1280, 256), BF16),
        ],
        compiler_params=PARAMS,
    )(volume, hleft, hright, codes)
    message = shape((592, 128), BF16)
    smoothed, left, right, face0, face1, res_left, res_right, peak = pl.pallas_call(
        forward_kernel,
        out_shape=(grid, message, message, plane, plane, strip, strip, shape((32, 128), F32)),
        in_specs=[vmem] * 8 + [smem],
        scratch_shapes=[
            pltpu.VMEM((2, 1280, 256), BF16),
            pltpu.VMEM(volume.shape, F32),
            pltpu.VMEM((2, 8, 256, 128), BF16),
        ],
        compiler_params=PARAMS,
    )(volume, low, high, following, partial, keys, weights, codes, stencil)
    hright = ring(left, "gy", -1)
    hleft = ring(right, "gy", 1)
    fhigh = ring(face0, "gz", -1)
    flow = ring(face1, "gz", 1)
    slab = shape((2640, 128), I16)
    smoothed, down, up, ahead, left, right = pl.pallas_call(
        functools.partial(complete_kernel, z_count, y_count),
        out_shape=(grid, slab, slab, shape((2064, 128), I16), strip, strip),
        in_specs=[vmem] * 9 + [smem],
        compiler_params=PARAMS,
    )(smoothed, flow, fhigh, hleft, hright, res_left, res_right, peak, codes, stencil)
    high = ring(down, "gz", -1)
    low = ring(up, "gz", 1)
    earlier = ring(ahead, "phase", 1)
    scratch = [
        pltpu.VMEM((24, 128), F32),
        pltpu.VMEM((24, 128), F32),
        pltpu.VMEM((3, 24, 128), F32),
        pltpu.VMEM((24, 128, 128), I16),
        pltpu.VMEM((24, 512, 128), BF16),
    ]
    partial = pl.pallas_call(
        functools.partial(inner_kernel, z_count, y_count),
        out_shape=grid,
        scratch_shapes=scratch + [pltpu.VMEM((2, 768, 256), BF16)],
        compiler_params=PARAMS,
    )(smoothed, codes)
    return pl.pallas_call(
        functools.partial(outer_kernel, z_count, y_count),
        out_shape=grid,
        in_specs=[vmem] * 8 + [smem],
        scratch_shapes=scratch + [pltpu.VMEM((2, 1792, 256), BF16)],
        compiler_params=PARAMS,
    )(partial, low, high, hleft, hright, left, right, earlier, stencil)


def solution(mesh):
    placed = (
        P("phase", None, "gz", "gy"),
        P("phase", "gz", "gy", None),
        P("phase", "gz", "gy", None),
        P(),
    )
    return jax.shard_map(
        body, mesh=mesh, in_specs=placed, out_specs=P("phase", None, "gz", "gy"), check_vma=False
    )
```

```python
import functools

import jax
import jax.numpy as jnp
from jax import lax
from jax.experimental import pallas as pl
from jax.experimental.pallas import tpu as pltpu
from jax.sharding import PartitionSpec as P

BS = 16
F32 = jnp.float32
BF16 = jnp.bfloat16
I32 = jnp.int32
I16 = jnp.int16
NONE = -4096


def iota(shape, dim, dtype=I32):
    return lax.broadcasted_iota(dtype, shape, dim)


def ring(cells, axis, by):
    count = lax.axis_size(axis)
    return lax.ppermute(cells, axis, [(i, (i + by) % count) for i in range(count)])


def onehot(hit):
    return jnp.where(hit, jnp.array(1, BF16), jnp.array(0, BF16))


def dot(left, right):
    return jnp.dot(left, right, preferred_element_type=F32)


def swap(cells, far):
    count = lax.axis_size("gy")
    step = -1 if far else 1
    pairs = [(i, (i + (step if i % 2 == 0 else -step)) % count) for i in range(count)]
    return lax.ppermute(cells, "gy", pairs)


def by_parity(first, second):
    return jnp.where(lax.axis_index("gy") % 2 == 1, first, second)


def spread_matrix():
    return onehot(iota((128, 2048), 0, I16) == (iota((1, 2048), 1) >> 4).astype(I16))


def strip_matrix():
    column = iota((1, 256), 1)
    right = column >> 7
    group = ((column & 127) >> 4) ^ (4 - 4 * right)
    wanted = group * 128 + (column & 15) + right * 112
    return onehot(iota((1024, 256), 0, I16) == wanted.astype(I16))


def displacements(codes):
    dx = (codes * 57) >> 9
    rest = codes - 9 * dx
    dz = (rest * 11) >> 5
    dy = rest - 3 * dz
    return dx - 1, dz - 1, dy - 1


def fraction(level):
    return (level + 1).astype(F32) / 5.0


def encode(values, inverse):
    share = values * inverse
    root = share * lax.rsqrt(jnp.abs(share) + 1e-30)
    return ((root * 32767.0 + 12582912.0) - 12582912.0).astype(I32).astype(I16)


def decode(coded, scale):
    count = coded.astype(F32)
    return count * jnp.abs(count) * (scale * (1.0 / (32767.0 * 32767.0)))


def scale_of(message, row):
    return jnp.exp2(message[row : row + 16, :].astype(F32)[2:3])


def pack_kernel(vol, mate, far):
    for h in range(2):
        tiles = [
            vol[i // 4, (i % 4) * BS : (i % 4 + 1) * BS, h * BS : (h + 1) * BS].reshape(256, 128)
            for i in range(8)
        ]
        strips = dot(jnp.concatenate(tiles, axis=1), strip_matrix())
        rows = slice(h * 256, (h + 1) * 256)
        left, right = strips[:, :128], strips[:, 128:]
        mate[rows, :] = by_parity(left, right).astype(BF16)
        far[rows, :] = by_parity(right, left).astype(BF16)


def pack_strips(tiles, p):
    chosen = strip_matrix()[p * 512 : (p + 1) * 512]
    return [dot(jnp.concatenate(half, axis=1), chosen) for half in tiles]


def mixed(first, second, p):
    low = iota(first.shape, first.ndim - 1) < 64
    return jnp.where(low, first, second) if p == 0 else jnp.where(low, second, first)


def slab_kernel(vol, mate, far, *outs):
    first, sides = outs[4:]
    first[...] = vol[0]
    for half in range(2):
        rows = slice(half * 256, (half + 1) * 256)
        theirs = [mate[rows, :].astype(F32), far[rows, :].astype(F32)]
        hleft, hright = by_parity(*theirs), by_parity(*theirs[::-1])
        for p in range(2):
            out = outs[p * 2 + half]
            cells = vol[p, :, half * BS : (half + 1) * BS, :]
            out[0:1024, :] = cells.reshape(1024, 128)
            cells = mixed(hleft, hright, p).astype(BF16)
            out[1024:1280, :] = cells
            sides[p, half] = cells


def near_kernel(
    z_count, y_count, vol, sides, shift, frac,
    gathered, keys, weights, codes, shifts, fracs, mask,
):
    rz = lax.axis_index("gz")
    ry = lax.axis_index("gy")
    both = [
        jnp.concatenate([part[0, 0].astype(F32), part[1, 0].astype(F32)], axis=1)
        for part in (shift, frac)
    ]
    at = iota((BS, 128), 0)
    codes[...] = jnp.where(at == 0, both[0], jnp.where(at == 1, both[1], 0.0)).astype(BF16)
    spread = dot(codes[...], spread_matrix())
    for i in range(8):
        shifts[i : i + 1, :] = spread[0:1, i * 256 : (i + 1) * 256]
        fracs[i : i + 1, :] = spread[1:2, i * 256 : (i + 1) * 256]
    dx, dz, dy = displacements(shifts[...].astype(I32))
    row = iota((8, 256), 0)
    lane = iota((8, 256), 1)
    bz = lane >> 7
    by = (lane >> 4) & 7
    yy = lane & 15
    bx = row & 3
    source_x = jnp.clip(bx + dx, 0, 3)
    source_z = jnp.clip(rz * 2 + bz + dz, 0, 2 * z_count - 1) - rz * 2 + 1
    source_y = jnp.clip(ry * 8 + by + dy, 0, 8 * y_count - 1) - ry * 8
    inside = (source_y >= 0) & (source_y < 8)
    keys[0] = jnp.where(inside, (source_x - bx + 1) * 4 + source_z, -1)
    keys[1] = source_y * BS + yy
    keys[2] = jnp.where(inside, -1, source_z)
    keys[3] = (jnp.where(source_y < 0, row >> 2, 1 - (row >> 2)) * 4 + source_x) * BS + yy
    levels = fracs[...].astype(I32)
    weights[0] = fraction(levels >> 4)
    weights[1] = fraction((levels >> 2) & 3)
    weights[2] = jnp.where(yy == 15, 0.0, fraction(levels & 3))

    def step(block):
        for p in range(2):

            def tile(xb, zb):
                xs = slice(xb * BS, (xb + 1) * BS)
                return vol[p, xs, (zb - 1) * BS : zb * BS, :].reshape(256, 128)

            i = p * 4 + block
            strips = [sides[p, 0], sides[p, 1]]
            gathered[i] = gather(i, keys, mask.at[i], tile, strips, (1, 2)).astype(BF16)

    for block in range(4):
        step(block)


def gather(i, keys, mask, tile, strips, z_blocks):
    here = [keys[k, i : i + 1, :] for k in range(4)]
    sublane = iota((128, 256), 0, I16)
    pieces = []

    def add(piece, hit, place):
        at = len(pieces) * 128
        mask[at : at + 128, :] = onehot(sublane == jnp.where(hit, place, NONE).astype(I16))
        pieces.append(piece)

    for d in range(3):
        xb = i % 4 + d - 1
        if not 0 <= xb < 4:
            continue
        for zb in z_blocks:
            add(tile(xb, zb), here[0] == d * 4 + zb, here[1])
    for k, zb in enumerate(z_blocks):
        add(strips[k], here[2] == zb, here[3])
    return dot(jnp.concatenate(pieces, axis=1), mask[0 : len(pieces) * 128, :])


def forward_kernel(p, coming, low, high, partial, keys, weights, stencil, *rest):
    if p == 1:
        before_res, before_smoothed, codes, *rest = rest
        smoothed, face0, face1, peak, mate, far, res_left, res_right, mask, res, strips_in = rest
    else:
        smoothed, face0, face1, peak, packed_res, packed_smoothed, mask, res, strips_in = rest
    s0, s1, s2, s3 = (stencil[k] for k in range(4))
    last_z = iota((1, BS, 128), 1) == BS - 1

    for block in range(4):
        xs = slice(block * BS, (block + 1) * BS)
        i = p * 4 + block

        def tile(xb, zb):
            return (low if zb == 0 else high)[xb * 256 : (xb + 1) * 256, :]

        strips = [slab[1024:1280, :] for slab in (low, high)]
        more = gather(i, keys, mask.at[block], tile, strips, (0, 3))
        gathered = partial[block].astype(F32) + more
        levels_here = [weights[k, i : i + 1, :] for k in range(3)]
        for half in range(2):
            part = slice(half * 128, (half + 1) * 128)
            zs = slice(half * BS, (half + 1) * BS)
            wx, wz, wy = (w[:, part].reshape(1, 1, 128) for w in levels_here)
            wz = jnp.where(last_z, 0.0, wz)
            cells = gathered[:, part].reshape(BS, BS, 128)
            cells = cells + wy * (pltpu.roll(cells, 127, 2) - cells)
            cells = cells + wz * (pltpu.roll(cells, BS - 1, 1) - cells)
            after = jnp.concatenate([cells[1:], cells[BS - 1 :]], axis=0)
            cells = cells + wx * (after - cells)
            cells = cells - coming[xs, zs, :].astype(F32)
            res[xs, zs, :] = cells
            strips_in[half, block] = cells.astype(BF16).reshape(256, 128)
            if half == 0:
                face0[xs, :] = cells[:, 0, :].astype(BF16)
            else:
                face1[xs, :] = cells[:, BS - 1, :].astype(BF16)

    packed = pack_strips([[strips_in[half, k] for k in range(4)] for half in range(2)], p)
    if p == 0:
        for half in range(2):
            packed_res[half] = packed[half].astype(BF16)
    else:
        messages = []
        group = iota((BS, 128), 1) & 15
        packed = [packed[half] + before_res[half].astype(F32) for half in range(2)]
        for side, edge, out in ((0, 0, res_left), (1, 15, res_right)):
            columns, edges = [], []
            for half in range(2):
                flat = packed[half][:, side * 128 : (side + 1) * 128]
                out[half * 256 : (half + 1) * 256, :] = flat.astype(BF16)
                cells = flat.reshape(BS, BS, 128)
                column = jnp.zeros((BS, 128), F32)
                for xi in range(BS):
                    turn = (xi - edge + 64 - 64 * side) % 128
                    plane = pltpu.roll(cells[xi], turn, 1) if turn else cells[xi]
                    column = jnp.where(group == xi, plane, column)
                columns.append(column)
                edges.append(cells[:, half * (BS - 1), :])
            messages.append(jnp.concatenate([codes[...].astype(F32)] + columns + edges, axis=0))
        mate[512:592, :] = by_parity(*messages).astype(BF16)
        far[512:592, :] = by_parity(*messages[::-1]).astype(BF16)

    zi = iota((32, 128), 0)
    lane = iota((32, 128), 1)

    def smooth(block, top):
        x0 = block * BS
        before = res[jnp.maximum(x0 - 1, 0)] * (block > 0).astype(F32)
        cells = res[x0]
        for xi in range(BS):
            if xi < BS - 1:
                after = res[x0 + xi + 1]
            else:
                after = res[jnp.minimum(x0 + BS, 63)] * (block < 3).astype(F32)
            top = jnp.maximum(top, jnp.abs(cells))
            z_low = jnp.where(zi == 0, 0.0, pltpu.roll(cells, 1, 0))
            z_high = jnp.where(zi == 31, 0.0, pltpu.roll(cells, 31, 0))
            y_low = jnp.where(lane == 0, 0.0, pltpu.roll(cells, 1, 1))
            y_high = jnp.where(lane == 127, 0.0, pltpu.roll(cells, 127, 1))
            value = s0 * cells + s1 * (before + after)
            value = value + s2 * (z_low + z_high) + s3 * (y_low + y_high)
            smoothed[x0 + xi] = value
            rounded = value.astype(BF16)
            rows = pl.ds(xi * BS, BS)
            strips_in[0, block, rows, :] = rounded[:BS]
            strips_in[1, block, rows, :] = rounded[BS:]
            before = cells
            cells = after
        return top

    peak[...] = lax.fori_loop(0, 4, smooth, jnp.zeros((32, 128), F32))
    packed = pack_strips([[strips_in[half, k] for k in range(4)] for half in range(2)], p)
    for half in range(2):
        if p == 0:
            packed_smoothed[half] = packed[half].astype(BF16)
        else:
            rows = slice(half * 256, (half + 1) * 256)
            cells = packed[half] + before_smoothed[half].astype(F32)
            mate[rows, :] = by_parity(cells[:, :128], cells[:, 128:]).astype(BF16)
            far[rows, :] = by_parity(cells[:, 128:], cells[:, :128]).astype(BF16)


def join_kernel(
    y_count, mate, far, res_left, res_right, peak0, peak1, stencil,
    hleft, hright, left, right, sides, parity, tops,
):
    ry = lax.axis_index("gy")
    s3 = stencil[3]
    theirs = [mate[...].astype(F32), far[...].astype(F32)]
    messages = [by_parity(*theirs), by_parity(*theirs[::-1])]
    hleft[...] = messages[0].astype(BF16)
    hright[...] = messages[1].astype(BF16)
    columns = [
        messages[0][528:560] * (ry > 0).astype(F32),
        messages[1][528:560] * (ry < y_count - 1).astype(F32),
    ]
    turned = pltpu.roll(columns[1], 127, 1)
    lane = iota((32, 128), 1)
    for odd in range(2):
        parity[odd] = s3 * jnp.where((lane & 1) == odd, columns[0], turned)
    group = iota((256, 128), 1) & 15
    strips = []
    for out, message, own, edge in (
        (left, messages[0], res_left, 15), (right, messages[1], res_right, 0)
    ):
        for half in range(2):
            rows = slice(half * 256, (half + 1) * 256)
            beside = pltpu.roll(own[rows, :].astype(F32), 79 if edge else 49, 1)
            cells = message[rows] + jnp.where(group == edge, s3 * beside, 0.0)
            out[rows, :] = cells.astype(BF16)
            strips.append(cells)
    inner = jnp.maximum(jnp.max(peak0[...]), jnp.max(peak1[...]))
    for cells in columns:
        inner = jnp.maximum(inner, jnp.max(jnp.abs(cells)))
    edges = [message[560:592] for message in messages]
    direct = jnp.array(1e-30, F32)
    for cells in (*strips, *edges):
        direct = jnp.maximum(direct, jnp.max(jnp.abs(cells)))
    tops[...] = jnp.where(iota((8, 128), 0) == 0, inner, direct)
    for half in range(2):
        part = slice(half * BS, (half + 1) * BS)
        for p in range(2):
            sides[p, half, 0:256, :] = mixed(strips[half], strips[2 + half], p)
            sides[p, half, 256:272, :] = mixed(edges[0][part], edges[1][part], p)


def power_of(z_count, tops, flow, fhigh, stencil):
    rz = lax.axis_index("gz")
    low = jnp.max(jnp.abs(flow[...].astype(F32))) * (rz > 0).astype(F32)
    high = jnp.max(jnp.abs(fhigh[...].astype(F32))) * (rz < z_count - 1).astype(F32)
    inner = jnp.maximum(tops[0:1, :], jnp.maximum(low, high))
    top = inner * (stencil[0] + 2.0 * (stencil[1] + stencil[2] + stencil[3]))
    top = jnp.maximum(top, tops[1:2, :])
    return jnp.ceil(jnp.log(top) * 1.4426950408889634)


def complete_kernel(
    p, z_count, partial, flow, fhigh, sides, parity, tops, codes, hleft, hright, stencil, *rest
):
    smoothed, down, up, *ahead = rest
    rz = lax.axis_index("gz")
    has_low = (rz > 0).astype(F32) * stencil[2]
    has_high = (rz < z_count - 1).astype(F32) * stencil[2]
    power = power_of(z_count, tops, flow, fhigh, stencil)
    inverse = 1.0 / jnp.exp2(power)
    tail = jnp.where(iota((BS, 128), 0) == 2, power, codes[...].astype(F32))
    tail = [tail] + [message[512:528, :].astype(F32) for message in (hleft, hright)]
    tail = jnp.concatenate(tail, axis=0).astype(I32).astype(I16)
    for half, out in enumerate((down, up)):
        out[1024:1296, :] = encode(sides[p, half], inverse)
        out[1296:1344, :] = tail
    for out in ahead:
        out[2048:2064, :] = tail[0:BS]
    lane = iota((32, 128), 1)
    at_edge = (lane == 0) | (lane == 127)
    zi = iota((BS, 128), 0)
    low_edge = zi == 0
    high_edge = zi == BS - 1

    def step(block, carry):
        i = p * 4 + block
        turn = (128 - i * BS) % 128
        sides_here = [pltpu.roll(parity[odd], turn, 1) for odd in range(2)]
        rows = pl.ds(pl.multiple_of(i * BS, BS), BS)
        lows = flow[rows, :].astype(F32) * has_low
        highs = fhigh[rows, :].astype(F32) * has_high
        for xi in range(BS):
            side = sides_here[xi & 1]
            if xi:
                side = pltpu.roll(side, 128 - xi, 1)
            x = block * BS + xi
            value = partial[x] + jnp.where(at_edge, side, 0.0)
            first = value[:BS] + jnp.where(low_edge, lows[xi : xi + 1], 0.0)
            second = value[BS:] + jnp.where(high_edge, highs[xi : xi + 1], 0.0)
            smoothed[x, 0:BS, :] = first
            smoothed[x, BS : 2 * BS, :] = second
            first = encode(first, inverse)
            second = encode(second, inverse)
            out_rows = pl.ds(pl.multiple_of(x * BS, BS), BS)
            down[out_rows, :] = first
            up[out_rows, :] = second
            for out in ahead:
                out[pl.ds(pl.multiple_of(x * 32, 32), BS), :] = first
                out[pl.ds(pl.multiple_of(x * 32 + BS, BS), BS), :] = second
        return carry

    lax.fori_loop(0, 4, step, 0)


def turned_warp(cells, wx, wy, wz):
    scaled = wy * cells
    cells = cells - scaled + pltpu.roll(scaled, 1, 2)
    scaled = wz * cells
    cells = cells - scaled + pltpu.roll(scaled, 1, 1)
    scaled = wx * cells[: BS - 1]
    zero = jnp.zeros((1, BS, 128), F32)
    cells = cells - jnp.concatenate([scaled, zero], axis=0) + jnp.concatenate([zero, scaled], axis=0)
    cells = cells.reshape(256, 128)
    high = cells.astype(BF16)
    return high, (cells - high.astype(F32)).astype(BF16)


def targets(z_count, y_count, shifts, fracs, p, turned, weights):
    rz = lax.axis_index("gz")
    ry = lax.axis_index("gy")
    dx, dz, dy = displacements(shifts[...].astype(I32))
    row = iota((BS, 128), 0)
    lane = iota((BS, 128), 1)
    yy = lane & 15
    if p is None:
        number, zb, by, count = row >> 1, 1 + (row & 1), lane >> 4, 16
    else:
        strip = row >= 8
        zb = jnp.where(strip, row & 3, 3 * (row & 1))
        number = p * 4 + jnp.where(strip, (lane >> 4) & 3, (row >> 1) & 3)
        from_left = (lane < 64) if p == 0 else (lane >= 64)
        by = jnp.where(strip, jnp.where(from_left, -1, 8), lane >> 4)
        count = 12
    bx = number & 3
    dest_z = rz * 2 + zb - 1
    dest_y = ry * 8 + by
    there = (dest_z >= 0) & (dest_z < 2 * z_count) & (dest_y >= 0) & (dest_y < 8 * y_count)
    source_x = jnp.clip(bx + dx, 0, 3)
    source_z = jnp.clip(dest_z + dz, 0, 2 * z_count - 1) - rz * 2
    source_y = jnp.clip(dest_y + dy, 0, 8 * y_count - 1) - ry * 8
    there = there & (source_z >= 0) & (source_z < 2) & (source_y >= 0) & (source_y < 8)
    target = ((number >> 2) * 4 + source_x) * 256 + source_z * 128 + source_y * BS + yy
    target = jnp.where(there, target, NONE).astype(F32)
    nobody = jnp.full((112, 128), float(NONE), F32)
    columns = jnp.concatenate([target, nobody], axis=0).T
    for r in range(count):
        turned[r] = jnp.broadcast_to(columns[:, r : r + 1], (128, 128)).astype(I16)
    levels = fracs[...].astype(I32)
    weights[0] = fraction(levels >> 4)
    weights[1] = fraction((levels >> 2) & 3)
    weights[2] = jnp.where(yy == 15, 0.0, fraction(levels & 3))


def strip_codes(p, zb, sources, half, shifts, fracs):
    lane = iota((1, 128), 1)
    picked = []
    for source, edge in zip(sources, (7, 0)):
        block = p * 64 + (((lane >> 4) & 3) * 2 + half) * 8 + edge
        hit = iota((128, 128), 0, I16) == block.astype(I16)
        picked.append(dot(source, onehot(hit)))
    cells = mixed(*picked, p)
    shifts[8 + zb : 9 + zb, :] = cells[0:1, :]
    fracs[8 + zb : 9 + zb, :] = cells[1:2, :]


def pull_all(count, tiles_of, strips, weights, pulled):
    last_z = iota((1, BS, 128), 1) == BS - 1

    def put(r, cells):
        wx, wz, wy = (weights[k, pl.ds(r, 1), :].reshape(1, 1, 128) for k in range(3))
        first, second = turned_warp(cells, wx, wy, jnp.where(last_z, 0.0, wz))
        pulled[r, 0:256, :] = first
        pulled[r, 256:512, :] = second

    def pull(i, carry):
        for k, cells in enumerate(tiles_of(i)):
            put(i * 2 + k, cells)
        return carry

    lax.fori_loop(0, count, pull, 0)
    for k, cells in enumerate(strips):
        put(count * 2 + k, cells)


def collect(i, base, turned, pulled, mask, strips):
    lanes = iota((128, 256), 1, I16) + jnp.array(i * 256, I16)
    pieces = []

    def add(r):
        at = len(pieces) * 128
        column = turned[r]
        column = jnp.concatenate([column, column], axis=1)
        mask[at : at + 128, :] = onehot(column == lanes)
        pieces.append(pulled[r])

    for d in range(3):
        if not 0 <= i % 4 + d - 1 < 4:
            continue
        for k in range(2):
            add((i - base + d - 1) * 2 + k)
    for r in strips:
        add(r)
    both = dot(jnp.concatenate(pieces, axis=1), mask[0 : len(pieces) * 128, :])
    return both[0:256] + both[256:512]


def inner_kernel(
    z_count, y_count, smoothed0, smoothed1, codes,
    out0, out1, shifts, fracs, weights, turned, pulled, mask,
):
    own = dot(codes[...], spread_matrix())
    for i in range(8):
        for half in range(2):
            part = slice(i * 256 + half * 128, i * 256 + half * 128 + 128)
            shifts[i * 2 + half : i * 2 + half + 1, :] = own[0:1, part]
            fracs[i * 2 + half : i * 2 + half + 1, :] = own[1:2, part]
    targets(z_count, y_count, shifts, fracs, None, turned, weights)
    for p, smoothed in enumerate((smoothed0, smoothed1)):

        def tiles_of(i):
            xs = pl.ds(pl.multiple_of(i * BS, BS), BS)
            return smoothed[xs, 0:BS, :], smoothed[xs, BS : 2 * BS, :]

        pull_all(4, tiles_of, (), weights.at[:, p * 8 : p * 8 + 8], pulled.at[p * 8 : p * 8 + 8])
    for i in range(8):
        p, block = divmod(i, 4)
        xs = slice(block * BS, (block + 1) * BS)
        total = collect(i, 0, turned, pulled, mask.at[i], ())
        for half in range(2):
            zs = slice(half * BS, (half + 1) * BS)
            cells = total[:, half * 128 : (half + 1) * 128].reshape(BS, BS, 128)
            if p == 0:
                out0[xs, zs, :] = cells
            else:
                out1[xs, zs, :] = cells - smoothed0[xs, zs, :]


def outer_kernel(
    p, z_count, y_count, partial, low, high, hleft, hright, left, right, stencil, *rest
):
    if p == 0:
        earlier, _, *rest = rest
    out, shifts, fracs, weights, turned, pulled, mask = rest
    rz = lax.axis_index("gz")
    s2 = stencil[2]
    has_low = (rz > 0).astype(F32) * s2
    has_high = (rz < z_count - 1).astype(F32) * s2
    shifts[...] = jnp.zeros((BS, 128), F32)
    fracs[...] = jnp.zeros((BS, 128), F32)
    spread = spread_matrix()[:, p * 1024 : (p + 1) * 1024]
    tails = [
        [slab[1296 + k * BS : 1312 + k * BS, :].astype(F32).astype(BF16) for k in range(3)]
        for slab in (low, high)
    ]
    for k, half in ((0, 1), (1, 0)):
        theirs = dot(tails[k][0], spread)
        for i in range(4):
            part = slice(i * 256 + half * 128, i * 256 + half * 128 + 128)
            shifts[i * 2 + k : i * 2 + k + 1, :] = theirs[0:1, part]
            fracs[i * 2 + k : i * 2 + k + 1, :] = theirs[1:2, part]
    beside = (hleft[512:528, :], hright[512:528, :])
    strip_codes(p, 0, tails[0][1:], 1, shifts, fracs)
    strip_codes(p, 1, beside, 0, shifts, fracs)
    strip_codes(p, 2, beside, 1, shifts, fracs)
    strip_codes(p, 3, tails[1][1:], 0, shifts, fracs)
    targets(z_count, y_count, shifts, fracs, p, turned, weights)
    low_scale = scale_of(low, 1296)
    high_scale = scale_of(high, 1296)
    zi = iota((1, BS, 128), 1)

    def with_row(cells, row, values):
        cells = cells.reshape(BS, BS, 128)
        return cells + jnp.where(zi == row, values.reshape(BS, 1, 128), 0.0)

    def both(first, second, rows):
        return mixed(first[rows, :].astype(F32), second[rows, :].astype(F32), p)

    def tiles_of(i):
        rows = pl.ds(pl.multiple_of(i * 256, 256), 256)
        return (
            decode(low[rows, :], low_scale).reshape(BS, BS, 128),
            decode(high[rows, :], high_scale).reshape(BS, BS, 128),
        )

    strips = [
        with_row(
            decode(low[1024:1280, :], low_scale), BS - 1, s2 * both(hleft, hright, slice(560, 576))
        ),
        with_row(
            both(left, right, slice(0, 256)), 0, has_low * decode(low[1280:1296, :], low_scale)
        ),
        with_row(
            both(left, right, slice(256, 512)),
            BS - 1,
            has_high * decode(high[1280:1296, :], high_scale),
        ),
        with_row(
            decode(high[1024:1280, :], high_scale), 0, s2 * both(hleft, hright, slice(576, 592))
        ),
    ]
    pull_all(4, tiles_of, strips, weights, pulled)
    for block in range(4):
        xs = slice(block * BS, (block + 1) * BS)
        total = collect(p * 4 + block, p * 4, turned, pulled, mask.at[block], range(8, 12))
        if p == 0:
            scale = scale_of(earlier, 2048)
            passed = decode(earlier[block * 512 : (block + 1) * 512, :], scale)
            passed = passed.reshape(BS, 2 * BS, 128)
        for half in range(2):
            zs = slice(half * BS, (half + 1) * BS)
            cells = total[:, half * 128 : (half + 1) * 128].reshape(BS, BS, 128)
            cells = cells + partial[xs, zs, :]
            if p == 0:
                cells = cells - passed[:, zs]
            out[0, xs, zs, :] = cells


PARAMS = pltpu.CompilerParams(vmem_limit_bytes=24 * 1024 * 1024)


def shape(dims, dtype):
    return jax.ShapeDtypeStruct(dims, dtype)


def call(kernel, out_shape, args, scratch=(), stencil=None, **more):
    specs = [
        pl.BlockSpec(memory_space=pltpu.SMEM if k == stencil else pltpu.VMEM)
        for k in range(len(args))
    ]
    more.setdefault("in_specs", specs)
    more.setdefault("compiler_params", PARAMS)
    return pl.pallas_call(kernel, out_shape=out_shape, scratch_shapes=list(scratch), **more)(*args)


def body(volume, shift_code, frac_code, stencil):
    z_count = lax.axis_size("gz")
    y_count = lax.axis_size("gy")
    strip = shape((512, 128), BF16)
    cube = shape(volume.shape[1:], F32)
    mate, far = call(
        pack_kernel,
        (strip, strip),
        (volume,),
    )
    far = swap(far, True)
    mate = swap(mate, False)
    slab = shape((1280, 128), BF16)
    down0, up0, down1, up1, first, sides = call(
        slab_kernel,
        (slab,) * 4 + (shape(volume.shape[1:], BF16), shape((2, 2, 256, 128), BF16)),
        (volume, mate, far),
    )
    highs = [ring(down0, "gz", -1)]
    lows = [ring(up0, "gz", 1)]
    highs.append(ring(down1, "gz", -1))
    lows.append(ring(up1, "gz", 1))
    following = ring(first, "phase", -1)
    gathered, keys, weights, codes = call(
        functools.partial(near_kernel, z_count, y_count),
        (
            shape((8, 256, 256), BF16),
            shape((4, 8, 256), I32),
            shape((3, 8, 256), F32),
            shape((BS, 128), BF16),
        ),
        (volume, sides, shift_code, frac_code),
        [
            pltpu.VMEM((8, 256), F32),
            pltpu.VMEM((8, 256), F32),
            pltpu.VMEM((8, 1024, 256), BF16),
        ],
    )
    scratch = [
        pltpu.VMEM((4, 1024, 256), BF16),
        pltpu.VMEM(volume.shape[1:], F32),
        pltpu.VMEM((2, 4, 256, 128), BF16),
    ]
    face = shape((64, 128), BF16)
    peak = shape((32, 128), F32)
    packed = shape((2, 256, 256), BF16)
    message = shape((592, 128), BF16)
    smoothed0, face00, face10, peak0, packed_res, packed_smoothed = call(
        functools.partial(forward_kernel, 0),
        (cube, face, face, peak, packed, packed),
        (volume[1], lows[0], highs[0], gathered[:4], keys, weights, stencil),
        scratch,
        stencil=6,
    )
    smoothed1, face01, face11, peak1, mate, far, res_left, res_right = call(
        functools.partial(forward_kernel, 1),
        (cube, face, face, peak, message, message, strip, strip),
        (
            following, lows[1], highs[1], gathered[4:], keys, weights, stencil,
            packed_res, packed_smoothed, codes,
        ),
        scratch,
        stencil=6,
    )
    far = swap(far, True)
    mate = swap(mate, False)
    fhigh = ring(jnp.concatenate([face00, face01]), "gz", -1)
    flow = ring(jnp.concatenate([face10, face11]), "gz", 1)
    hleft, hright, left, right, sides, parity, tops = call(
        functools.partial(join_kernel, y_count),
        (
            message, message, strip, strip,
            shape((2, 2, 272, 128), F32), shape((2, 32, 128), F32), shape((8, 128), F32),
        ),
        (mate, far, res_left, res_right, peak0, peak1, stencil),
        stencil=6,
    )
    slab = shape((1344, 128), I16)
    common = (flow, fhigh, sides, parity, tops, codes, hleft, hright, stencil)
    smoothed1, down1, up1, ahead = call(
        functools.partial(complete_kernel, 1, z_count),
        (cube, slab, slab, shape((2064, 128), I16)),
        (smoothed1, *common),
        stencil=9,
    )
    high1 = ring(down1, "gz", -1)
    low1 = ring(up1, "gz", 1)
    earlier = ring(ahead, "phase", 1)
    smoothed0, down0, up0 = call(
        functools.partial(complete_kernel, 0, z_count),
        (cube, slab, slab),
        (smoothed0, *common),
        stencil=9,
    )
    high0 = ring(down0, "gz", -1)
    low0 = ring(up0, "gz", 1)

    def scratch_of(rows, tiles, width):
        return [
            pltpu.VMEM((BS, 128), F32),
            pltpu.VMEM((BS, 128), F32),
            pltpu.VMEM((3, BS, 128), F32),
            pltpu.VMEM((BS, 128, 128), I16),
            pltpu.VMEM((rows, 512, 128), BF16),
            pltpu.VMEM((tiles, width, 256), BF16),
        ]

    partial0, partial1 = call(
        functools.partial(inner_kernel, z_count, y_count),
        (cube, cube),
        (smoothed0, smoothed1, codes),
        scratch_of(16, 8, 768),
    )
    vmem = pl.BlockSpec(memory_space=pltpu.VMEM)
    smem = pl.BlockSpec(memory_space=pltpu.SMEM)
    anywhere = pl.BlockSpec(memory_space=pl.ANY)
    out = ()
    for p, partial, low, high in ((1, partial1, low1, high1), (0, partial0, low0, high0)):
        more = () if p == 1 else (earlier, out)
        out = call(
            functools.partial(outer_kernel, p, z_count, y_count),
            shape(volume.shape, F32),
            (partial, low, high, hleft, hright, left, right, stencil, *more),
            scratch_of(12, 4, 1280),
            grid=(1,),
            in_specs=[vmem] * 7 + [smem] + ([vmem, anywhere] if more else []),
            out_specs=pl.BlockSpec((1,) + volume.shape[1:], functools.partial(phase_block, p)),
            input_output_aliases={9: 0} if more else {},
        )
    return out


def phase_block(p, step):
    return p, 0, 0, 0


def solution(mesh):
    placed = (
        P("phase", None, "gz", "gy"),
        P("phase", "gz", "gy", None),
        P("phase", "gz", "gy", None),
        P(),
    )
    return jax.shard_map(
        body, mesh=mesh, in_specs=placed, out_specs=P("phase", None, "gz", "gy"), check_vma=False
    )
```

```python
import functools

import jax
import jax.numpy as jnp
from jax import lax
from jax.experimental import pallas as pl
from jax.experimental.pallas import tpu as pltpu
from jax.sharding import PartitionSpec as P

BS = 16
F32 = jnp.float32
BF16 = jnp.bfloat16
I32 = jnp.int32
I16 = jnp.int16
NONE = -4096


def iota(shape, dim, dtype=I32):
    return lax.broadcasted_iota(dtype, shape, dim)


def ring(cells, axis, by):
    count = lax.axis_size(axis)
    return lax.ppermute(cells, axis, [(i, (i + by) % count) for i in range(count)])


def onehot(hit):
    return jnp.where(hit, jnp.array(1, BF16), jnp.array(0, BF16))


def dot(left, right):
    return jnp.dot(left, right, preferred_element_type=F32)


def swap(cells, far):
    count = lax.axis_size("gy")
    step = -1 if far else 1
    pairs = [(i, (i + (step if i % 2 == 0 else -step)) % count) for i in range(count)]
    return lax.ppermute(cells, "gy", pairs)


def by_parity(first, second):
    return jnp.where(lax.axis_index("gy") % 2 == 1, first, second)


def spread_matrix():
    return onehot(iota((128, 2048), 0, I16) == (iota((1, 2048), 1) >> 4).astype(I16))


def strip_matrix():
    column = iota((1, 256), 1)
    right = column >> 7
    group = ((column & 127) >> 4) ^ (4 - 4 * right)
    wanted = group * 128 + (column & 15) + right * 112
    return onehot(iota((1024, 256), 0, I16) == wanted.astype(I16))


def displacements(codes):
    dx = (codes * 57) >> 9
    rest = codes - 9 * dx
    dz = (rest * 11) >> 5
    dy = rest - 3 * dz
    return dx - 1, dz - 1, dy - 1


def fraction(level):
    return (level + 1).astype(F32) / 5.0


def encode(values, inverse):
    share = values * inverse
    root = share * lax.rsqrt(jnp.abs(share) + 1e-30)
    return ((root * 32767.0 + 12582912.0) - 12582912.0).astype(I32).astype(I16)


def decode(coded, scale):
    count = coded.astype(F32)
    return count * jnp.abs(count) * (scale * (1.0 / (32767.0 * 32767.0)))


def scale_of(message, row):
    return jnp.exp2(message[row : row + 16, :].astype(F32)[2:3])


def pack_kernel(vol, mate, far):
    for h in range(2):
        tiles = [
            vol[i // 4, (i % 4) * BS : (i % 4 + 1) * BS, h * BS : (h + 1) * BS].reshape(256, 128)
            for i in range(8)
        ]
        strips = dot(jnp.concatenate(tiles, axis=1), strip_matrix())
        rows = slice(h * 256, (h + 1) * 256)
        left, right = strips[:, :128], strips[:, 128:]
        mate[rows, :] = by_parity(left, right).astype(BF16)
        far[rows, :] = by_parity(right, left).astype(BF16)


def pack_strips(tiles, p):
    chosen = strip_matrix()[p * 512 : (p + 1) * 512]
    return [dot(jnp.concatenate(half, axis=1), chosen) for half in tiles]


def mixed(first, second, p):
    low = iota(first.shape, first.ndim - 1) < 64
    return jnp.where(low, first, second) if p == 0 else jnp.where(low, second, first)


def slab_kernel(vol, mate, far, *outs):
    first, sides = outs[4:]
    first[...] = vol[0]
    for half in range(2):
        rows = slice(half * 256, (half + 1) * 256)
        theirs = [mate[rows, :].astype(F32), far[rows, :].astype(F32)]
        hleft, hright = by_parity(*theirs), by_parity(*theirs[::-1])
        for p in range(2):
            out = outs[p * 2 + half]
            cells = vol[p, :, half * BS : (half + 1) * BS, :]
            out[0:1024, :] = cells.reshape(1024, 128)
            cells = mixed(hleft, hright, p).astype(BF16)
            out[1024:1280, :] = cells
            sides[p, half] = cells


def near_kernel(
    z_count, y_count, vol, sides, shift, frac,
    gathered, keys, weights, codes, shifts, fracs, mask,
):
    rz = lax.axis_index("gz")
    ry = lax.axis_index("gy")
    both = [
        jnp.concatenate([part[0, 0].astype(F32), part[1, 0].astype(F32)], axis=1)
        for part in (shift, frac)
    ]
    at = iota((BS, 128), 0)
    codes[...] = jnp.where(at == 0, both[0], jnp.where(at == 1, both[1], 0.0)).astype(BF16)
    spread = dot(codes[...], spread_matrix())
    for i in range(8):
        shifts[i : i + 1, :] = spread[0:1, i * 256 : (i + 1) * 256]
        fracs[i : i + 1, :] = spread[1:2, i * 256 : (i + 1) * 256]
    dx, dz, dy = displacements(shifts[...].astype(I32))
    row = iota((8, 256), 0)
    lane = iota((8, 256), 1)
    bz = lane >> 7
    by = (lane >> 4) & 7
    yy = lane & 15
    bx = row & 3
    source_x = jnp.clip(bx + dx, 0, 3)
    source_z = jnp.clip(rz * 2 + bz + dz, 0, 2 * z_count - 1) - rz * 2 + 1
    source_y = jnp.clip(ry * 8 + by + dy, 0, 8 * y_count - 1) - ry * 8
    inside = (source_y >= 0) & (source_y < 8)
    keys[0] = jnp.where(inside, (source_x - bx + 1) * 4 + source_z, -1)
    keys[1] = source_y * BS + yy
    keys[2] = jnp.where(inside, -1, source_z)
    keys[3] = (jnp.where(source_y < 0, row >> 2, 1 - (row >> 2)) * 4 + source_x) * BS + yy
    levels = fracs[...].astype(I32)
    weights[0] = fraction(levels >> 4)
    weights[1] = fraction((levels >> 2) & 3)
    weights[2] = jnp.where(yy == 15, 0.0, fraction(levels & 3))

    def step(block):
        for p in range(2):

            def tile(xb, zb):
                xs = slice(xb * BS, (xb + 1) * BS)
                return vol[p, xs, (zb - 1) * BS : zb * BS, :].reshape(256, 128)

            i = p * 4 + block
            strips = [sides[p, 0], sides[p, 1]]
            gathered[i] = gather(i, keys, mask.at[i], tile, strips, (1, 2)).astype(BF16)

    for block in range(4):
        step(block)


def gather(i, keys, mask, tile, strips, z_blocks):
    here = [keys[k, i : i + 1, :] for k in range(4)]
    sublane = iota((128, 256), 0, I16)
    pieces = []

    def add(piece, hit, place):
        at = len(pieces) * 128
        mask[at : at + 128, :] = onehot(sublane == jnp.where(hit, place, NONE).astype(I16))
        pieces.append(piece)

    for d in range(3):
        xb = i % 4 + d - 1
        if not 0 <= xb < 4:
            continue
        for zb in z_blocks:
            add(tile(xb, zb), here[0] == d * 4 + zb, here[1])
    for k, zb in enumerate(z_blocks):
        add(strips[k], here[2] == zb, here[3])
    return dot(jnp.concatenate(pieces, axis=1), mask[0 : len(pieces) * 128, :])


def forward_kernel(p, coming, low, high, partial, keys, weights, stencil, *rest):
    if p == 0:
        _, *rest = rest
    if p == 1:
        before_res, before_smoothed, codes, *rest = rest
        smoothed, face0, face1, peak, mate, far, res_left, res_right, mask, res, strips_in = rest
    else:
        smoothed, face0, face1, peak, packed_res, packed_smoothed, mask, res, strips_in = rest
    s0, s1, s2, s3 = (stencil[k] for k in range(4))
    last_z = iota((1, BS, 128), 1) == BS - 1

    for block in range(4):
        xs = slice(block * BS, (block + 1) * BS)
        i = p * 4 + block

        def tile(xb, zb):
            return (low if zb == 0 else high)[xb * 256 : (xb + 1) * 256, :]

        strips = [slab[1024:1280, :] for slab in (low, high)]
        more = gather(i, keys, mask.at[block], tile, strips, (0, 3))
        gathered = partial[block].astype(F32) + more
        levels_here = [weights[k, i : i + 1, :] for k in range(3)]
        for half in range(2):
            part = slice(half * 128, (half + 1) * 128)
            zs = slice(half * BS, (half + 1) * BS)
            wx, wz, wy = (w[:, part].reshape(1, 1, 128) for w in levels_here)
            wz = jnp.where(last_z, 0.0, wz)
            cells = gathered[:, part].reshape(BS, BS, 128)
            cells = cells + wy * (pltpu.roll(cells, 127, 2) - cells)
            cells = cells + wz * (pltpu.roll(cells, BS - 1, 1) - cells)
            after = jnp.concatenate([cells[1:], cells[BS - 1 :]], axis=0)
            cells = cells + wx * (after - cells)
            cells = cells - coming[xs, zs, :].astype(F32)
            res[xs, zs, :] = cells
            strips_in[half, block] = cells.astype(BF16).reshape(256, 128)
            if half == 0:
                face0[xs, :] = cells[:, 0, :].astype(BF16)
            else:
                face1[xs, :] = cells[:, BS - 1, :].astype(BF16)

    packed = pack_strips([[strips_in[half, k] for k in range(4)] for half in range(2)], p)
    if p == 0:
        for half in range(2):
            packed_res[half] = packed[half].astype(BF16)
    else:
        messages = []
        group = iota((BS, 128), 1) & 15
        packed = [packed[half] + before_res[half].astype(F32) for half in range(2)]
        for side, edge, out in ((0, 0, res_left), (1, 15, res_right)):
            columns, edges = [], []
            for half in range(2):
                flat = packed[half][:, side * 128 : (side + 1) * 128]
                out[half * 256 : (half + 1) * 256, :] = flat.astype(BF16)
                cells = flat.reshape(BS, BS, 128)
                column = jnp.zeros((BS, 128), F32)
                for xi in range(BS):
                    turn = (xi - edge + 64 - 64 * side) % 128
                    plane = pltpu.roll(cells[xi], turn, 1) if turn else cells[xi]
                    column = jnp.where(group == xi, plane, column)
                columns.append(column)
                edges.append(cells[:, half * (BS - 1), :])
            messages.append(jnp.concatenate([codes[...].astype(F32)] + columns + edges, axis=0))
        mate[512:592, :] = by_parity(*messages).astype(BF16)
        far[512:592, :] = by_parity(*messages[::-1]).astype(BF16)

    zi = iota((32, 128), 0)
    lane = iota((32, 128), 1)

    def smooth(block, top):
        x0 = block * BS
        before = res[jnp.maximum(x0 - 1, 0)] * (block > 0).astype(F32)
        cells = res[x0]
        for xi in range(BS):
            if xi < BS - 1:
                after = res[x0 + xi + 1]
            else:
                after = res[jnp.minimum(x0 + BS, 63)] * (block < 3).astype(F32)
            top = jnp.maximum(top, jnp.abs(cells))
            z_low = jnp.where(zi == 0, 0.0, pltpu.roll(cells, 1, 0))
            z_high = jnp.where(zi == 31, 0.0, pltpu.roll(cells, 31, 0))
            y_low = jnp.where(lane == 0, 0.0, pltpu.roll(cells, 1, 1))
            y_high = jnp.where(lane == 127, 0.0, pltpu.roll(cells, 127, 1))
            value = s0 * cells + s1 * (before + after)
            value = value + s2 * (z_low + z_high) + s3 * (y_low + y_high)
            smoothed[x0 + xi] = value
            rounded = value.astype(BF16)
            rows = pl.ds(xi * BS, BS)
            strips_in[0, block, rows, :] = rounded[:BS]
            strips_in[1, block, rows, :] = rounded[BS:]
            before = cells
            cells = after
        return top

    peak[...] = lax.fori_loop(0, 4, smooth, jnp.zeros((32, 128), F32))
    packed = pack_strips([[strips_in[half, k] for k in range(4)] for half in range(2)], p)
    for half in range(2):
        if p == 0:
            packed_smoothed[half] = packed[half].astype(BF16)
        else:
            rows = slice(half * 256, (half + 1) * 256)
            cells = packed[half] + before_smoothed[half].astype(F32)
            mate[rows, :] = by_parity(cells[:, :128], cells[:, 128:]).astype(BF16)
            far[rows, :] = by_parity(cells[:, 128:], cells[:, :128]).astype(BF16)


def join_kernel(
    y_count, mate, far, res_left, res_right, peak0, peak1, stencil,
    hleft, hright, left, right, sides, parity, tops,
):
    ry = lax.axis_index("gy")
    s3 = stencil[3]
    theirs = [mate[...].astype(F32), far[...].astype(F32)]
    messages = [by_parity(*theirs), by_parity(*theirs[::-1])]
    hleft[...] = messages[0].astype(BF16)
    hright[...] = messages[1].astype(BF16)
    columns = [
        messages[0][528:560] * (ry > 0).astype(F32),
        messages[1][528:560] * (ry < y_count - 1).astype(F32),
    ]
    turned = pltpu.roll(columns[1], 127, 1)
    lane = iota((32, 128), 1)
    for odd in range(2):
        parity[odd] = s3 * jnp.where((lane & 1) == odd, columns[0], turned)
    group = iota((256, 128), 1) & 15
    strips = []
    for out, message, own, edge in (
        (left, messages[0], res_left, 15), (right, messages[1], res_right, 0)
    ):
        for half in range(2):
            rows = slice(half * 256, (half + 1) * 256)
            beside = pltpu.roll(own[rows, :].astype(F32), 79 if edge else 49, 1)
            cells = message[rows] + jnp.where(group == edge, s3 * beside, 0.0)
            out[rows, :] = cells.astype(BF16)
            strips.append(cells)
    inner = jnp.maximum(jnp.max(peak0[...]), jnp.max(peak1[...]))
    for cells in columns:
        inner = jnp.maximum(inner, jnp.max(jnp.abs(cells)))
    edges = [message[560:592] for message in messages]
    direct = jnp.array(1e-30, F32)
    for cells in (*strips, *edges):
        direct = jnp.maximum(direct, jnp.max(jnp.abs(cells)))
    tops[...] = jnp.where(iota((8, 128), 0) == 0, inner, direct)
    for half in range(2):
        part = slice(half * BS, (half + 1) * BS)
        for p in range(2):
            sides[p, half, 0:256, :] = mixed(strips[half], strips[2 + half], p)
            sides[p, half, 256:272, :] = mixed(edges[0][part], edges[1][part], p)


def power_of(z_count, tops, flow, fhigh, stencil):
    rz = lax.axis_index("gz")
    low = jnp.max(jnp.abs(flow[...].astype(F32))) * (rz > 0).astype(F32)
    high = jnp.max(jnp.abs(fhigh[...].astype(F32))) * (rz < z_count - 1).astype(F32)
    inner = jnp.maximum(tops[0:1, :], jnp.maximum(low, high))
    top = inner * (stencil[0] + 2.0 * (stencil[1] + stencil[2] + stencil[3]))
    top = jnp.maximum(top, tops[1:2, :])
    return jnp.ceil(jnp.log(top) * 1.4426950408889634)


def complete_kernel(
    p, z_count, partial, flow, fhigh, sides, parity, tops, codes, hleft, hright, stencil, *rest
):
    smoothed, down, up, *ahead = rest
    rz = lax.axis_index("gz")
    has_low = (rz > 0).astype(F32) * stencil[2]
    has_high = (rz < z_count - 1).astype(F32) * stencil[2]
    power = power_of(z_count, tops, flow, fhigh, stencil)
    inverse = 1.0 / jnp.exp2(power)
    tail = jnp.where(iota((BS, 128), 0) == 2, power, codes[...].astype(F32))
    tail = [tail] + [message[512:528, :].astype(F32) for message in (hleft, hright)]
    tail = jnp.concatenate(tail, axis=0).astype(I32).astype(I16)
    for half, out in enumerate((down, up)):
        out[1024:1296, :] = encode(sides[p, half], inverse)
        out[1296:1344, :] = tail
    for out in ahead:
        out[2048:2064, :] = tail[0:BS]
    lane = iota((32, 128), 1)
    at_edge = (lane == 0) | (lane == 127)
    zi = iota((BS, 128), 0)
    low_edge = zi == 0
    high_edge = zi == BS - 1

    def step(block, carry):
        i = p * 4 + block
        turn = (128 - i * BS) % 128
        sides_here = [pltpu.roll(parity[odd], turn, 1) for odd in range(2)]
        rows = pl.ds(pl.multiple_of(i * BS, BS), BS)
        lows = flow[rows, :].astype(F32) * has_low
        highs = fhigh[rows, :].astype(F32) * has_high
        for xi in range(BS):
            side = sides_here[xi & 1]
            if xi:
                side = pltpu.roll(side, 128 - xi, 1)
            x = block * BS + xi
            value = partial[x] + jnp.where(at_edge, side, 0.0)
            first = value[:BS] + jnp.where(low_edge, lows[xi : xi + 1], 0.0)
            second = value[BS:] + jnp.where(high_edge, highs[xi : xi + 1], 0.0)
            smoothed[x, 0:BS, :] = first
            smoothed[x, BS : 2 * BS, :] = second
            first = encode(first, inverse)
            second = encode(second, inverse)
            out_rows = pl.ds(pl.multiple_of(x * BS, BS), BS)
            down[out_rows, :] = first
            up[out_rows, :] = second
            for out in ahead:
                out[pl.ds(pl.multiple_of(x * 32, 32), BS), :] = first
                out[pl.ds(pl.multiple_of(x * 32 + BS, BS), BS), :] = second
        return carry

    lax.fori_loop(0, 4, step, 0)


def turned_warp(cells, wx, wy, wz):
    scaled = wy * cells
    cells = cells - scaled + pltpu.roll(scaled, 1, 2)
    scaled = wz * cells
    cells = cells - scaled + pltpu.roll(scaled, 1, 1)
    scaled = wx * cells[: BS - 1]
    zero = jnp.zeros((1, BS, 128), F32)
    cells = cells - jnp.concatenate([scaled, zero], axis=0) + jnp.concatenate([zero, scaled], axis=0)
    cells = cells.reshape(256, 128)
    high = cells.astype(BF16)
    return high, (cells - high.astype(F32)).astype(BF16)


def targets(z_count, y_count, shifts, fracs, p, turned, weights):
    rz = lax.axis_index("gz")
    ry = lax.axis_index("gy")
    dx, dz, dy = displacements(shifts[...].astype(I32))
    row = iota((BS, 128), 0)
    lane = iota((BS, 128), 1)
    yy = lane & 15
    if p is None:
        number, zb, by, count = row >> 1, 1 + (row & 1), lane >> 4, 16
    else:
        strip = row >= 8
        zb = jnp.where(strip, row & 3, 3 * (row & 1))
        number = p * 4 + jnp.where(strip, (lane >> 4) & 3, (row >> 1) & 3)
        from_left = (lane < 64) if p == 0 else (lane >= 64)
        by = jnp.where(strip, jnp.where(from_left, -1, 8), lane >> 4)
        count = 12
    bx = number & 3
    dest_z = rz * 2 + zb - 1
    dest_y = ry * 8 + by
    there = (dest_z >= 0) & (dest_z < 2 * z_count) & (dest_y >= 0) & (dest_y < 8 * y_count)
    source_x = jnp.clip(bx + dx, 0, 3)
    source_z = jnp.clip(dest_z + dz, 0, 2 * z_count - 1) - rz * 2
    source_y = jnp.clip(dest_y + dy, 0, 8 * y_count - 1) - ry * 8
    there = there & (source_z >= 0) & (source_z < 2) & (source_y >= 0) & (source_y < 8)
    target = ((number >> 2) * 4 + source_x) * 256 + source_z * 128 + source_y * BS + yy
    target = jnp.where(there, target, NONE).astype(F32)
    nobody = jnp.full((112, 128), float(NONE), F32)
    columns = jnp.concatenate([target, nobody], axis=0).T
    for r in range(count):
        turned[r] = jnp.broadcast_to(columns[:, r : r + 1], (128, 128)).astype(I16)
    levels = fracs[...].astype(I32)
    weights[0] = fraction(levels >> 4)
    weights[1] = fraction((levels >> 2) & 3)
    weights[2] = jnp.where(yy == 15, 0.0, fraction(levels & 3))


def strip_codes(p, zb, sources, half, shifts, fracs):
    lane = iota((1, 128), 1)
    picked = []
    for source, edge in zip(sources, (7, 0)):
        block = p * 64 + (((lane >> 4) & 3) * 2 + half) * 8 + edge
        hit = iota((128, 128), 0, I16) == block.astype(I16)
        picked.append(dot(source, onehot(hit)))
    cells = mixed(*picked, p)
    shifts[8 + zb : 9 + zb, :] = cells[0:1, :]
    fracs[8 + zb : 9 + zb, :] = cells[1:2, :]


def pull_all(count, tiles_of, strips, weights, pulled):
    last_z = iota((1, BS, 128), 1) == BS - 1

    def put(r, cells):
        wx, wz, wy = (weights[k, pl.ds(r, 1), :].reshape(1, 1, 128) for k in range(3))
        first, second = turned_warp(cells, wx, wy, jnp.where(last_z, 0.0, wz))
        pulled[r, 0:256, :] = first
        pulled[r, 256:512, :] = second

    def pull(i, carry):
        for k, cells in enumerate(tiles_of(i)):
            put(i * 2 + k, cells)
        return carry

    lax.fori_loop(0, count, pull, 0)
    for k, cells in enumerate(strips):
        put(count * 2 + k, cells)


def tiles_for(i, base, strips):
    near = [d for d in (-1, 0, 1) if 0 <= i % 4 + d < 4]
    return [(i - base + d) * 2 + k for d in near for k in range(2)] + list(strips)


def plan_masks(i, base, turned, mask, strips):
    lanes = iota((128, 256), 1, I16) + jnp.array(i * 256, I16)
    for at, r in enumerate(tiles_for(i, base, strips)):
        column = turned[r]
        column = jnp.concatenate([column, column], axis=1)
        mask[at * 128 : (at + 1) * 128, :] = onehot(column == lanes)


def collect(i, base, pulled, mask, strips):
    rows = tiles_for(i, base, strips)
    pieces = jnp.concatenate([pulled[r] for r in rows], axis=1)
    both = dot(pieces, mask[0 : len(rows) * 128, :])
    return both[0:256] + both[256:512]


def plan_kernel(z_count, y_count, codes, mask, weights, shifts, fracs, turned):
    own = dot(codes[...], spread_matrix())
    for i in range(8):
        for half in range(2):
            part = slice(i * 256 + half * 128, i * 256 + half * 128 + 128)
            shifts[i * 2 + half : i * 2 + half + 1, :] = own[0:1, part]
            fracs[i * 2 + half : i * 2 + half + 1, :] = own[1:2, part]
    targets(z_count, y_count, shifts, fracs, None, turned, weights)
    for i in range(8):
        plan_masks(i, 0, turned, mask.at[i], ())


def inner_kernel(smoothed0, smoothed1, mask, weights, out0, out1, pulled):
    for p, smoothed in enumerate((smoothed0, smoothed1)):

        def tiles_of(i):
            xs = pl.ds(pl.multiple_of(i * BS, BS), BS)
            return smoothed[xs, 0:BS, :], smoothed[xs, BS : 2 * BS, :]

        pull_all(4, tiles_of, (), weights.at[:, p * 8 : p * 8 + 8], pulled.at[p * 8 : p * 8 + 8])
    for i in range(8):
        p, block = divmod(i, 4)
        xs = slice(block * BS, (block + 1) * BS)
        total = collect(i, 0, pulled, mask.at[i], ())
        for half in range(2):
            zs = slice(half * BS, (half + 1) * BS)
            cells = total[:, half * 128 : (half + 1) * 128].reshape(BS, BS, 128)
            if p == 0:
                out0[xs, zs, :] = cells
            else:
                out1[xs, zs, :] = cells - smoothed0[xs, zs, :]


def outer_kernel(
    p, z_count, y_count, partial, low, high, hleft, hright, left, right, stencil, *rest
):
    if p == 0:
        earlier, _, *rest = rest
    out, shifts, fracs, weights, turned, pulled, mask = rest
    rz = lax.axis_index("gz")
    s2 = stencil[2]
    has_low = (rz > 0).astype(F32) * s2
    has_high = (rz < z_count - 1).astype(F32) * s2
    shifts[...] = jnp.zeros((BS, 128), F32)
    fracs[...] = jnp.zeros((BS, 128), F32)
    spread = spread_matrix()[:, p * 1024 : (p + 1) * 1024]
    tails = [
        [slab[1296 + k * BS : 1312 + k * BS, :].astype(F32).astype(BF16) for k in range(3)]
        for slab in (low, high)
    ]
    for k, half in ((0, 1), (1, 0)):
        theirs = dot(tails[k][0], spread)
        for i in range(4):
            part = slice(i * 256 + half * 128, i * 256 + half * 128 + 128)
            shifts[i * 2 + k : i * 2 + k + 1, :] = theirs[0:1, part]
            fracs[i * 2 + k : i * 2 + k + 1, :] = theirs[1:2, part]
    beside = (hleft[512:528, :], hright[512:528, :])
    strip_codes(p, 0, tails[0][1:], 1, shifts, fracs)
    strip_codes(p, 1, beside, 0, shifts, fracs)
    strip_codes(p, 2, beside, 1, shifts, fracs)
    strip_codes(p, 3, tails[1][1:], 0, shifts, fracs)
    targets(z_count, y_count, shifts, fracs, p, turned, weights)
    low_scale = scale_of(low, 1296)
    high_scale = scale_of(high, 1296)
    zi = iota((1, BS, 128), 1)

    def with_row(cells, row, values):
        cells = cells.reshape(BS, BS, 128)
        return cells + jnp.where(zi == row, values.reshape(BS, 1, 128), 0.0)

    def both(first, second, rows):
        return mixed(first[rows, :].astype(F32), second[rows, :].astype(F32), p)

    def tiles_of(i):
        rows = pl.ds(pl.multiple_of(i * 256, 256), 256)
        return (
            decode(low[rows, :], low_scale).reshape(BS, BS, 128),
            decode(high[rows, :], high_scale).reshape(BS, BS, 128),
        )

    strips = [
        with_row(
            decode(low[1024:1280, :], low_scale), BS - 1, s2 * both(hleft, hright, slice(560, 576))
        ),
        with_row(
            both(left, right, slice(0, 256)), 0, has_low * decode(low[1280:1296, :], low_scale)
        ),
        with_row(
            both(left, right, slice(256, 512)),
            BS - 1,
            has_high * decode(high[1280:1296, :], high_scale),
        ),
        with_row(
            decode(high[1024:1280, :], high_scale), 0, s2 * both(hleft, hright, slice(576, 592))
        ),
    ]
    pull_all(4, tiles_of, strips, weights, pulled)
    for block in range(4):
        xs = slice(block * BS, (block + 1) * BS)
        plan_masks(p * 4 + block, p * 4, turned, mask.at[block], range(8, 12))
        total = collect(p * 4 + block, p * 4, pulled, mask.at[block], range(8, 12))
        if p == 0:
            scale = scale_of(earlier, 2048)
            passed = decode(earlier[block * 512 : (block + 1) * 512, :], scale)
            passed = passed.reshape(BS, 2 * BS, 128)
        for half in range(2):
            zs = slice(half * BS, (half + 1) * BS)
            cells = total[:, half * 128 : (half + 1) * 128].reshape(BS, BS, 128)
            cells = cells + partial[xs, zs, :]
            if p == 0:
                cells = cells - passed[:, zs]
            out[0, xs, zs, :] = cells


PARAMS = pltpu.CompilerParams(vmem_limit_bytes=24 * 1024 * 1024)


def shape(dims, dtype):
    return jax.ShapeDtypeStruct(dims, dtype)


def call(kernel, out_shape, args, scratch=(), stencil=None, **more):
    specs = [
        pl.BlockSpec(memory_space=pltpu.SMEM if k == stencil else pltpu.VMEM)
        for k in range(len(args))
    ]
    more.setdefault("in_specs", specs)
    more.setdefault("compiler_params", PARAMS)
    return pl.pallas_call(kernel, out_shape=out_shape, scratch_shapes=list(scratch), **more)(*args)


def body(volume, shift_code, frac_code, stencil):
    z_count = lax.axis_size("gz")
    y_count = lax.axis_size("gy")
    strip = shape((512, 128), BF16)
    cube = shape(volume.shape[1:], F32)
    mate, far = call(
        pack_kernel,
        (strip, strip),
        (volume,),
    )
    far = swap(far, True)
    mate = swap(mate, False)
    slab = shape((1280, 128), BF16)
    down0, up0, down1, up1, first, sides = call(
        slab_kernel,
        (slab,) * 4 + (shape(volume.shape[1:], BF16), shape((2, 2, 256, 128), BF16)),
        (volume, mate, far),
    )
    highs = [ring(down0, "gz", -1)]
    lows = [ring(up0, "gz", 1)]
    highs.append(ring(down1, "gz", -1))
    lows.append(ring(up1, "gz", 1))
    following = ring(first, "phase", -1)
    gathered, keys, weights, codes = call(
        functools.partial(near_kernel, z_count, y_count),
        (
            shape((8, 256, 256), BF16),
            shape((4, 8, 256), I32),
            shape((3, 8, 256), F32),
            shape((BS, 128), BF16),
        ),
        (volume, sides, shift_code, frac_code),
        [
            pltpu.VMEM((8, 256), F32),
            pltpu.VMEM((8, 256), F32),
            pltpu.VMEM((8, 1024, 256), BF16),
        ],
    )
    mask_in, weights_in = call(
        functools.partial(plan_kernel, z_count, y_count),
        (shape((8, 768, 256), BF16), shape((3, BS, 128), F32)),
        (codes,),
        [
            pltpu.VMEM((BS, 128), F32),
            pltpu.VMEM((BS, 128), F32),
            pltpu.VMEM((BS, 128, 128), I16),
        ],
    )
    scratch = [
        pltpu.VMEM((4, 1024, 256), BF16),
        pltpu.VMEM(volume.shape[1:], F32),
        pltpu.VMEM((2, 4, 256, 128), BF16),
    ]
    face = shape((64, 128), BF16)
    peak = shape((32, 128), F32)
    packed = shape((2, 256, 256), BF16)
    message = shape((592, 128), BF16)
    smoothed0, face00, face10, peak0, packed_res, packed_smoothed = call(
        functools.partial(forward_kernel, 0),
        (cube, face, face, peak, packed, packed),
        (volume[1], lows[0], highs[0], gathered[:4], keys, weights, stencil, weights_in),
        scratch,
        stencil=6,
    )
    smoothed1, face01, face11, peak1, mate, far, res_left, res_right = call(
        functools.partial(forward_kernel, 1),
        (cube, face, face, peak, message, message, strip, strip),
        (
            following, lows[1], highs[1], gathered[4:], keys, weights, stencil,
            packed_res, packed_smoothed, codes,
        ),
        scratch,
        stencil=6,
    )
    far = swap(far, True)
    mate = swap(mate, False)
    fhigh = ring(jnp.concatenate([face00, face01]), "gz", -1)
    flow = ring(jnp.concatenate([face10, face11]), "gz", 1)
    hleft, hright, left, right, sides, parity, tops = call(
        functools.partial(join_kernel, y_count),
        (
            message, message, strip, strip,
            shape((2, 2, 272, 128), F32), shape((2, 32, 128), F32), shape((8, 128), F32),
        ),
        (mate, far, res_left, res_right, peak0, peak1, stencil),
        stencil=6,
    )
    slab = shape((1344, 128), I16)
    common = (flow, fhigh, sides, parity, tops, codes, hleft, hright, stencil)
    smoothed1, down1, up1, ahead = call(
        functools.partial(complete_kernel, 1, z_count),
        (cube, slab, slab, shape((2064, 128), I16)),
        (smoothed1, *common),
        stencil=9,
    )
    high1 = ring(down1, "gz", -1)
    low1 = ring(up1, "gz", 1)
    earlier = ring(ahead, "phase", 1)
    smoothed0, down0, up0 = call(
        functools.partial(complete_kernel, 0, z_count),
        (cube, slab, slab),
        (smoothed0, *common),
        stencil=9,
    )
    high0 = ring(down0, "gz", -1)
    low0 = ring(up0, "gz", 1)

    def scratch_of(rows, tiles, width):
        return [
            pltpu.VMEM((BS, 128), F32),
            pltpu.VMEM((BS, 128), F32),
            pltpu.VMEM((3, BS, 128), F32),
            pltpu.VMEM((BS, 128, 128), I16),
            pltpu.VMEM((rows, 512, 128), BF16),
            pltpu.VMEM((tiles, width, 256), BF16),
        ]

    partial0, partial1 = call(
        inner_kernel,
        (cube, cube),
        (smoothed0, smoothed1, mask_in, weights_in),
        [pltpu.VMEM((16, 512, 128), BF16)],
    )
    vmem = pl.BlockSpec(memory_space=pltpu.VMEM)
    smem = pl.BlockSpec(memory_space=pltpu.SMEM)
    anywhere = pl.BlockSpec(memory_space=pl.ANY)
    out = ()
    for p, partial, low, high in ((1, partial1, low1, high1), (0, partial0, low0, high0)):
        more = () if p == 1 else (earlier, out)
        out = call(
            functools.partial(outer_kernel, p, z_count, y_count),
            shape(volume.shape, F32),
            (partial, low, high, hleft, hright, left, right, stencil, *more),
            scratch_of(12, 4, 1280),
            grid=(1,),
            in_specs=[vmem] * 7 + [smem] + ([vmem, anywhere] if more else []),
            out_specs=pl.BlockSpec((1,) + volume.shape[1:], functools.partial(phase_block, p)),
            input_output_aliases={9: 0} if more else {},
        )
    return out


def phase_block(p, step):
    return p, 0, 0, 0


def solution(mesh):
    placed = (
        P("phase", None, "gz", "gy"),
        P("phase", "gz", "gy", None),
        P("phase", "gz", "gy", None),
        P(),
    )
    return jax.shard_map(
        body, mesh=mesh, in_specs=placed, out_specs=P("phase", None, "gz", "gy"), check_vma=False
    )
```

```python
import functools

import jax
import jax.numpy as jnp
from jax import lax
from jax.experimental import pallas as pl
from jax.experimental.pallas import tpu as pltpu
from jax.sharding import PartitionSpec as P

BS = 16
F32 = jnp.float32
BF16 = jnp.bfloat16
I32 = jnp.int32
I16 = jnp.int16
NONE = -4096


def iota(shape, dim, dtype=I32):
    return lax.broadcasted_iota(dtype, shape, dim)


def ring(cells, axis, by):
    count = lax.axis_size(axis)
    return lax.ppermute(cells, axis, [(i, (i + by) % count) for i in range(count)])


def onehot(hit):
    return jnp.where(hit, jnp.array(1, BF16), jnp.array(0, BF16))


def dot(left, right):
    return jnp.dot(left, right, preferred_element_type=F32)


def swap(cells, far):
    count = lax.axis_size("gy")
    step = -1 if far else 1
    pairs = [(i, (i + (step if i % 2 == 0 else -step)) % count) for i in range(count)]
    return lax.ppermute(cells, "gy", pairs)


def by_parity(first, second):
    return jnp.where(lax.axis_index("gy") % 2 == 1, first, second)


def spread_matrix():
    return onehot(iota((128, 2048), 0, I16) == (iota((1, 2048), 1) >> 4).astype(I16))


def strip_matrix():
    column = iota((1, 256), 1)
    right = column >> 7
    group = ((column & 127) >> 4) ^ (4 - 4 * right)
    wanted = group * 128 + (column & 15) + right * 112
    return onehot(iota((1024, 256), 0, I16) == wanted.astype(I16))


def displacements(codes):
    dx = (codes * 57) >> 9
    rest = codes - 9 * dx
    dz = (rest * 11) >> 5
    dy = rest - 3 * dz
    return dx - 1, dz - 1, dy - 1


def fraction(level):
    return (level + 1).astype(F32) / 5.0


def encode(values, inverse):
    share = values * inverse
    root = share * lax.rsqrt(jnp.abs(share) + 1e-30)
    return ((root * 32767.0 + 12582912.0) - 12582912.0).astype(I32).astype(I16)


def decode(coded, scale):
    count = coded.astype(F32)
    return count * jnp.abs(count) * (scale * (1.0 / (32767.0 * 32767.0)))


def scale_of(message, row):
    return jnp.exp2(message[row : row + 16, :].astype(F32)[2:3])


def pack_kernel(vol, mate, far):
    for h in range(2):
        tiles = [
            vol[i // 4, (i % 4) * BS : (i % 4 + 1) * BS, h * BS : (h + 1) * BS].reshape(256, 128)
            for i in range(8)
        ]
        strips = dot(jnp.concatenate(tiles, axis=1), strip_matrix())
        rows = slice(h * 256, (h + 1) * 256)
        left, right = strips[:, :128], strips[:, 128:]
        mate[rows, :] = by_parity(left, right).astype(BF16)
        far[rows, :] = by_parity(right, left).astype(BF16)


def pack_strips(tiles, p):
    chosen = strip_matrix()[p * 512 : (p + 1) * 512]
    return [dot(jnp.concatenate(half, axis=1), chosen) for half in tiles]


def mixed(first, second, p):
    low = iota(first.shape, first.ndim - 1) < 64
    return jnp.where(low, first, second) if p == 0 else jnp.where(low, second, first)


def slab_kernel(vol, mate, far, *outs):
    first, sides = outs[4:]
    first[...] = vol[0]
    for half in range(2):
        rows = slice(half * 256, (half + 1) * 256)
        theirs = [mate[rows, :].astype(F32), far[rows, :].astype(F32)]
        hleft, hright = by_parity(*theirs), by_parity(*theirs[::-1])
        for p in range(2):
            out = outs[p * 2 + half]
            cells = vol[p, :, half * BS : (half + 1) * BS, :]
            out[0:1024, :] = cells.reshape(1024, 128)
            cells = mixed(hleft, hright, p).astype(BF16)
            out[1024:1280, :] = cells
            sides[p, half] = cells


def near_kernel(
    z_count, y_count, vol, sides, shift, frac,
    gathered, keys, weights, codes, shifts, fracs, mask,
):
    rz = lax.axis_index("gz")
    ry = lax.axis_index("gy")
    both = [
        jnp.concatenate([part[0, 0].astype(F32), part[1, 0].astype(F32)], axis=1)
        for part in (shift, frac)
    ]
    at = iota((BS, 128), 0)
    codes[...] = jnp.where(at == 0, both[0], jnp.where(at == 1, both[1], 0.0)).astype(BF16)
    spread = dot(codes[...], spread_matrix())
    for i in range(8):
        shifts[i : i + 1, :] = spread[0:1, i * 256 : (i + 1) * 256]
        fracs[i : i + 1, :] = spread[1:2, i * 256 : (i + 1) * 256]
    dx, dz, dy = displacements(shifts[...].astype(I32))
    row = iota((8, 256), 0)
    lane = iota((8, 256), 1)
    bz = lane >> 7
    by = (lane >> 4) & 7
    yy = lane & 15
    bx = row & 3
    source_x = jnp.clip(bx + dx, 0, 3)
    source_z = jnp.clip(rz * 2 + bz + dz, 0, 2 * z_count - 1) - rz * 2 + 1
    source_y = jnp.clip(ry * 8 + by + dy, 0, 8 * y_count - 1) - ry * 8
    inside = (source_y >= 0) & (source_y < 8)
    keys[0] = jnp.where(inside, (source_x - bx + 1) * 4 + source_z, -1)
    keys[1] = source_y * BS + yy
    keys[2] = jnp.where(inside, -1, source_z)
    keys[3] = (jnp.where(source_y < 0, row >> 2, 1 - (row >> 2)) * 4 + source_x) * BS + yy
    levels = fracs[...].astype(I32)
    weights[0] = fraction(levels >> 4)
    weights[1] = fraction((levels >> 2) & 3)
    weights[2] = jnp.where(yy == 15, 0.0, fraction(levels & 3))

    def step(block):
        for p in range(2):

            def tile(xb, zb):
                xs = slice(xb * BS, (xb + 1) * BS)
                return vol[p, xs, (zb - 1) * BS : zb * BS, :].reshape(256, 128)

            i = p * 4 + block
            strips = [sides[p, 0], sides[p, 1]]
            gathered[i] = gather(i, keys, mask.at[i], tile, strips, (1, 2)).astype(BF16)

    for block in range(4):
        step(block)


def gather(i, keys, mask, tile, strips, z_blocks):
    here = [keys[k, i : i + 1, :] for k in range(4)]
    sublane = iota((128, 256), 0, I16)
    pieces = []

    def add(piece, hit, place):
        at = len(pieces) * 128
        mask[at : at + 128, :] = onehot(sublane == jnp.where(hit, place, NONE).astype(I16))
        pieces.append(piece)

    for d in range(3):
        xb = i % 4 + d - 1
        if not 0 <= xb < 4:
            continue
        for zb in z_blocks:
            add(tile(xb, zb), here[0] == d * 4 + zb, here[1])
    for k, zb in enumerate(z_blocks):
        add(strips[k], here[2] == zb, here[3])
    return dot(jnp.concatenate(pieces, axis=1), mask[0 : len(pieces) * 128, :])


def forward_kernel(p, coming, low, high, partial, keys, weights, stencil, *rest):
    if p == 0:
        _, *rest = rest
    if p == 1:
        before_res, before_smoothed, codes, *rest = rest
        smoothed, face0, face1, peak, mate, far, res_left, res_right, mask, res, strips_in = rest
    else:
        smoothed, face0, face1, peak, packed_res, packed_smoothed, mask, res, strips_in = rest
    s0, s1, s2, s3 = (stencil[k] for k in range(4))
    last_z = iota((1, BS, 128), 1) == BS - 1

    for block in range(4):
        xs = slice(block * BS, (block + 1) * BS)
        i = p * 4 + block

        def tile(xb, zb):
            return (low if zb == 0 else high)[xb * 256 : (xb + 1) * 256, :]

        strips = [slab[1024:1280, :] for slab in (low, high)]
        more = gather(i, keys, mask.at[block], tile, strips, (0, 3))
        gathered = partial[block].astype(F32) + more
        levels_here = [weights[k, i : i + 1, :] for k in range(3)]
        for half in range(2):
            part = slice(half * 128, (half + 1) * 128)
            zs = slice(half * BS, (half + 1) * BS)
            wx, wz, wy = (w[:, part].reshape(1, 1, 128) for w in levels_here)
            wz = jnp.where(last_z, 0.0, wz)
            cells = gathered[:, part].reshape(BS, BS, 128)
            cells = cells + wy * (pltpu.roll(cells, 127, 2) - cells)
            cells = cells + wz * (pltpu.roll(cells, BS - 1, 1) - cells)
            after = jnp.concatenate([cells[1:], cells[BS - 1 :]], axis=0)
            cells = cells + wx * (after - cells)
            cells = cells - coming[xs, zs, :].astype(F32)
            res[xs, zs, :] = cells
            strips_in[half, block] = cells.astype(BF16).reshape(256, 128)
            if half == 0:
                face0[xs, :] = cells[:, 0, :].astype(BF16)
            else:
                face1[xs, :] = cells[:, BS - 1, :].astype(BF16)

    packed = pack_strips([[strips_in[half, k] for k in range(4)] for half in range(2)], p)
    if p == 0:
        for half in range(2):
            packed_res[half] = packed[half].astype(BF16)
    else:
        messages = []
        group = iota((BS, 128), 1) & 15
        packed = [packed[half] + before_res[half].astype(F32) for half in range(2)]
        for side, edge, out in ((0, 0, res_left), (1, 15, res_right)):
            columns, edges = [], []
            for half in range(2):
                flat = packed[half][:, side * 128 : (side + 1) * 128]
                out[half * 256 : (half + 1) * 256, :] = flat.astype(BF16)
                cells = flat.reshape(BS, BS, 128)
                column = jnp.zeros((BS, 128), F32)
                for xi in range(BS):
                    turn = (xi - edge + 64 - 64 * side) % 128
                    plane = pltpu.roll(cells[xi], turn, 1) if turn else cells[xi]
                    column = jnp.where(group == xi, plane, column)
                columns.append(column)
                edges.append(cells[:, half * (BS - 1), :])
            messages.append(jnp.concatenate([codes[...].astype(F32)] + columns + edges, axis=0))
        mate[512:592, :] = by_parity(*messages).astype(BF16)
        far[512:592, :] = by_parity(*messages[::-1]).astype(BF16)

    zi = iota((32, 128), 0)
    lane = iota((32, 128), 1)

    def smooth(block, top):
        x0 = block * BS
        before = res[x0 - 1] if block else jnp.zeros((32, 128), F32)
        cells = res[x0]
        for xi in range(BS):
            if xi < BS - 1:
                after = res[x0 + xi + 1]
            else:
                after = res[x0 + BS] if block < 3 else jnp.zeros((32, 128), F32)
            top = jnp.maximum(top, jnp.abs(cells))
            z_low = jnp.where(zi == 0, 0.0, pltpu.roll(cells, 1, 0))
            z_high = jnp.where(zi == 31, 0.0, pltpu.roll(cells, 31, 0))
            y_low = jnp.where(lane == 0, 0.0, pltpu.roll(cells, 1, 1))
            y_high = jnp.where(lane == 127, 0.0, pltpu.roll(cells, 127, 1))
            value = s0 * cells + s1 * (before + after)
            value = value + s2 * (z_low + z_high) + s3 * (y_low + y_high)
            smoothed[x0 + xi] = value
            rounded = value.astype(BF16)
            rows = pl.ds(xi * BS, BS)
            strips_in[0, block, rows, :] = rounded[:BS]
            strips_in[1, block, rows, :] = rounded[BS:]
            before = cells
            cells = after
        return top

    top = jnp.zeros((32, 128), F32)
    for block in range(4):
        top = smooth(block, top)
    peak[...] = top
    packed = pack_strips([[strips_in[half, k] for k in range(4)] for half in range(2)], p)
    for half in range(2):
        if p == 0:
            packed_smoothed[half] = packed[half].astype(BF16)
        else:
            rows = slice(half * 256, (half + 1) * 256)
            cells = packed[half] + before_smoothed[half].astype(F32)
            mate[rows, :] = by_parity(cells[:, :128], cells[:, 128:]).astype(BF16)
            far[rows, :] = by_parity(cells[:, 128:], cells[:, :128]).astype(BF16)


def join_kernel(
    y_count, mate, far, res_left, res_right, peak0, peak1, stencil,
    hleft, hright, left, right, sides, parity, tops,
):
    ry = lax.axis_index("gy")
    s3 = stencil[3]
    theirs = [mate[...].astype(F32), far[...].astype(F32)]
    messages = [by_parity(*theirs), by_parity(*theirs[::-1])]
    hleft[...] = messages[0].astype(BF16)
    hright[...] = messages[1].astype(BF16)
    columns = [
        messages[0][528:560] * (ry > 0).astype(F32),
        messages[1][528:560] * (ry < y_count - 1).astype(F32),
    ]
    turned = pltpu.roll(columns[1], 127, 1)
    lane = iota((32, 128), 1)
    for odd in range(2):
        parity[odd] = s3 * jnp.where((lane & 1) == odd, columns[0], turned)
    group = iota((256, 128), 1) & 15
    strips = []
    for out, message, own, edge in (
        (left, messages[0], res_left, 15), (right, messages[1], res_right, 0)
    ):
        for half in range(2):
            rows = slice(half * 256, (half + 1) * 256)
            beside = pltpu.roll(own[rows, :].astype(F32), 79 if edge else 49, 1)
            cells = message[rows] + jnp.where(group == edge, s3 * beside, 0.0)
            out[rows, :] = cells.astype(BF16)
            strips.append(cells)
    inner = jnp.maximum(jnp.max(peak0[...]), jnp.max(peak1[...]))
    for cells in columns:
        inner = jnp.maximum(inner, jnp.max(jnp.abs(cells)))
    edges = [message[560:592] for message in messages]
    direct = jnp.array(1e-30, F32)
    for cells in (*strips, *edges):
        direct = jnp.maximum(direct, jnp.max(jnp.abs(cells)))
    tops[...] = jnp.where(iota((8, 128), 0) == 0, inner, direct)
    for half in range(2):
        part = slice(half * BS, (half + 1) * BS)
        for p in range(2):
            sides[p, half, 0:256, :] = mixed(strips[half], strips[2 + half], p)
            sides[p, half, 256:272, :] = mixed(edges[0][part], edges[1][part], p)


def power_of(z_count, tops, flow, fhigh, stencil):
    rz = lax.axis_index("gz")
    low = jnp.max(jnp.abs(flow[...].astype(F32))) * (rz > 0).astype(F32)
    high = jnp.max(jnp.abs(fhigh[...].astype(F32))) * (rz < z_count - 1).astype(F32)
    inner = jnp.maximum(tops[0:1, :], jnp.maximum(low, high))
    top = inner * (stencil[0] + 2.0 * (stencil[1] + stencil[2] + stencil[3]))
    top = jnp.maximum(top, tops[1:2, :])
    return jnp.ceil(jnp.log(top) * 1.4426950408889634)


def complete_kernel(
    p, z_count, partial, flow, fhigh, sides, parity, tops, codes, hleft, hright, stencil, *rest
):
    smoothed, down, up, *ahead = rest
    rz = lax.axis_index("gz")
    has_low = (rz > 0).astype(F32) * stencil[2]
    has_high = (rz < z_count - 1).astype(F32) * stencil[2]
    power = power_of(z_count, tops, flow, fhigh, stencil)
    inverse = 1.0 / jnp.exp2(power)
    tail = jnp.where(iota((BS, 128), 0) == 2, power, codes[...].astype(F32))
    tail = [tail] + [message[512:528, :].astype(F32) for message in (hleft, hright)]
    tail = jnp.concatenate(tail, axis=0).astype(I32).astype(I16)
    for half, out in enumerate((down, up)):
        out[1024:1296, :] = encode(sides[p, half], inverse)
        out[1296:1344, :] = tail
    for out in ahead:
        out[2048:2064, :] = tail[0:BS]
    lane = iota((32, 128), 1)
    at_edge = (lane == 0) | (lane == 127)
    zi = iota((BS, 128), 0)
    low_edge = zi == 0
    high_edge = zi == BS - 1

    def step(block):
        i = p * 4 + block
        turn = (128 - i * BS) % 128
        sides_here = [pltpu.roll(parity[odd], turn, 1) for odd in range(2)]
        rows = slice(i * BS, (i + 1) * BS)
        lows = flow[rows, :].astype(F32) * has_low
        highs = fhigh[rows, :].astype(F32) * has_high
        for xi in range(BS):
            side = sides_here[xi & 1]
            if xi:
                side = pltpu.roll(side, 128 - xi, 1)
            x = block * BS + xi
            value = partial[x] + jnp.where(at_edge, side, 0.0)
            first = value[:BS] + jnp.where(low_edge, lows[xi : xi + 1], 0.0)
            second = value[BS:] + jnp.where(high_edge, highs[xi : xi + 1], 0.0)
            smoothed[x, 0:BS, :] = first
            smoothed[x, BS : 2 * BS, :] = second
            first = encode(first, inverse)
            second = encode(second, inverse)
            out_rows = slice(x * BS, (x + 1) * BS)
            down[out_rows, :] = first
            up[out_rows, :] = second
            for out in ahead:
                out[x * 32 : x * 32 + BS, :] = first
                out[x * 32 + BS : x * 32 + 2 * BS, :] = second

    for block in range(4):
        step(block)


def turned_warp(cells, wx, wy, wz):
    scaled = wy * cells
    cells = cells - scaled + pltpu.roll(scaled, 1, 2)
    scaled = wz * cells
    cells = cells - scaled + pltpu.roll(scaled, 1, 1)
    scaled = wx * cells[: BS - 1]
    zero = jnp.zeros((1, BS, 128), F32)
    cells = cells - jnp.concatenate([scaled, zero], axis=0) + jnp.concatenate([zero, scaled], axis=0)
    cells = cells.reshape(256, 128)
    high = cells.astype(BF16)
    return high, (cells - high.astype(F32)).astype(BF16)


def targets(z_count, y_count, shifts, fracs, p, turned, weights):
    rz = lax.axis_index("gz")
    ry = lax.axis_index("gy")
    dx, dz, dy = displacements(shifts[...].astype(I32))
    row = iota((BS, 128), 0)
    lane = iota((BS, 128), 1)
    yy = lane & 15
    if p is None:
        number, zb, by, count = row >> 1, 1 + (row & 1), lane >> 4, 16
    else:
        strip = row >= 8
        zb = jnp.where(strip, row & 3, 3 * (row & 1))
        number = p * 4 + jnp.where(strip, (lane >> 4) & 3, (row >> 1) & 3)
        from_left = (lane < 64) if p == 0 else (lane >= 64)
        by = jnp.where(strip, jnp.where(from_left, -1, 8), lane >> 4)
        count = 12
    bx = number & 3
    dest_z = rz * 2 + zb - 1
    dest_y = ry * 8 + by
    there = (dest_z >= 0) & (dest_z < 2 * z_count) & (dest_y >= 0) & (dest_y < 8 * y_count)
    source_x = jnp.clip(bx + dx, 0, 3)
    source_z = jnp.clip(dest_z + dz, 0, 2 * z_count - 1) - rz * 2
    source_y = jnp.clip(dest_y + dy, 0, 8 * y_count - 1) - ry * 8
    there = there & (source_z >= 0) & (source_z < 2) & (source_y >= 0) & (source_y < 8)
    target = ((number >> 2) * 4 + source_x) * 256 + source_z * 128 + source_y * BS + yy
    target = jnp.where(there, target, NONE).astype(F32)
    nobody = jnp.full((112, 128), float(NONE), F32)
    columns = jnp.concatenate([target, nobody], axis=0).T
    for r in range(count):
        turned[r] = jnp.broadcast_to(columns[:, r : r + 1], (128, 128)).astype(I16)
    levels = fracs[...].astype(I32)
    weights[0] = fraction(levels >> 4)
    weights[1] = fraction((levels >> 2) & 3)
    weights[2] = jnp.where(yy == 15, 0.0, fraction(levels & 3))


def strip_codes(p, zb, sources, half, shifts, fracs):
    lane = iota((1, 128), 1)
    picked = []
    for source, edge in zip(sources, (7, 0)):
        block = p * 64 + (((lane >> 4) & 3) * 2 + half) * 8 + edge
        hit = iota((128, 128), 0, I16) == block.astype(I16)
        picked.append(dot(source, onehot(hit)))
    cells = mixed(*picked, p)
    shifts[8 + zb : 9 + zb, :] = cells[0:1, :]
    fracs[8 + zb : 9 + zb, :] = cells[1:2, :]


def pull_all(count, tiles_of, strips, weights, pulled):
    last_z = iota((1, BS, 128), 1) == BS - 1

    def put(r, cells):
        wx, wz, wy = (weights[k, r : r + 1, :].reshape(1, 1, 128) for k in range(3))
        first, second = turned_warp(cells, wx, wy, jnp.where(last_z, 0.0, wz))
        pulled[r, 0:256, :] = first
        pulled[r, 256:512, :] = second

    for k, cells in enumerate(strips):
        put(count * 2 + k, cells)
    for i in range(count):
        for k, cells in enumerate(tiles_of(i)):
            put(i * 2 + k, cells)


def tiles_for(i, base, strips):
    near = [d for d in (-1, 0, 1) if 0 <= i % 4 + d < 4]
    return [(i - base + d) * 2 + k for d in near for k in range(2)] + list(strips)


def plan_masks(i, base, turned, mask, strips):
    lanes = iota((128, 256), 1, I16) + jnp.array(i * 256, I16)
    for at, r in enumerate(tiles_for(i, base, strips)):
        column = turned[r]
        column = jnp.concatenate([column, column], axis=1)
        mask[at * 128 : (at + 1) * 128, :] = onehot(column == lanes)


def collect(i, base, pulled, mask, strips):
    rows = tiles_for(i, base, strips)
    pieces = jnp.concatenate([pulled[r] for r in rows], axis=1)
    both = dot(pieces, mask[0 : len(rows) * 128, :])
    return both[0:256] + both[256:512]


def plan_kernel(z_count, y_count, codes, mask, weights, shifts, fracs, turned):
    own = dot(codes[...], spread_matrix())
    for i in range(8):
        for half in range(2):
            part = slice(i * 256 + half * 128, i * 256 + half * 128 + 128)
            shifts[i * 2 + half : i * 2 + half + 1, :] = own[0:1, part]
            fracs[i * 2 + half : i * 2 + half + 1, :] = own[1:2, part]
    targets(z_count, y_count, shifts, fracs, None, turned, weights)
    for i in range(8):
        plan_masks(i, 0, turned, mask.at[i], ())


def inner_kernel(smoothed0, smoothed1, mask, weights, out0, out1, pulled):
    for p, smoothed in enumerate((smoothed0, smoothed1)):

        def tiles_of(i):
            xs = slice(i * BS, (i + 1) * BS)
            return smoothed[xs, 0:BS, :], smoothed[xs, BS : 2 * BS, :]

        pull_all(4, tiles_of, (), weights.at[:, p * 8 : p * 8 + 8], pulled.at[p * 8 : p * 8 + 8])
    for i in range(8):
        p, block = divmod(i, 4)
        xs = slice(block * BS, (block + 1) * BS)
        total = collect(i, 0, pulled, mask.at[i], ())
        for half in range(2):
            zs = slice(half * BS, (half + 1) * BS)
            cells = total[:, half * 128 : (half + 1) * 128].reshape(BS, BS, 128)
            if p == 0:
                out0[xs, zs, :] = cells
            else:
                out1[xs, zs, :] = cells - smoothed0[xs, zs, :]


def outer_kernel(
    p, z_count, y_count, partial, low, high, hleft, hright, left, right, stencil, *rest
):
    if p == 0:
        earlier, _, *rest = rest
    out, shifts, fracs, weights, turned, pulled, mask = rest
    rz = lax.axis_index("gz")
    s2 = stencil[2]
    has_low = (rz > 0).astype(F32) * s2
    has_high = (rz < z_count - 1).astype(F32) * s2
    shifts[...] = jnp.zeros((BS, 128), F32)
    fracs[...] = jnp.zeros((BS, 128), F32)
    spread = spread_matrix()[:, p * 1024 : (p + 1) * 1024]
    tails = [
        [slab[1296 + k * BS : 1312 + k * BS, :].astype(F32).astype(BF16) for k in range(3)]
        for slab in (low, high)
    ]
    for k, half in ((0, 1), (1, 0)):
        theirs = dot(tails[k][0], spread)
        for i in range(4):
            part = slice(i * 256 + half * 128, i * 256 + half * 128 + 128)
            shifts[i * 2 + k : i * 2 + k + 1, :] = theirs[0:1, part]
            fracs[i * 2 + k : i * 2 + k + 1, :] = theirs[1:2, part]
    beside = (hleft[512:528, :], hright[512:528, :])
    strip_codes(p, 0, tails[0][1:], 1, shifts, fracs)
    strip_codes(p, 1, beside, 0, shifts, fracs)
    strip_codes(p, 2, beside, 1, shifts, fracs)
    strip_codes(p, 3, tails[1][1:], 0, shifts, fracs)
    targets(z_count, y_count, shifts, fracs, p, turned, weights)
    low_scale = scale_of(low, 1296)
    high_scale = scale_of(high, 1296)
    zi = iota((1, BS, 128), 1)

    def with_row(cells, row, values):
        cells = cells.reshape(BS, BS, 128)
        return cells + jnp.where(zi == row, values.reshape(BS, 1, 128), 0.0)

    def both(first, second, rows):
        return mixed(first[rows, :].astype(F32), second[rows, :].astype(F32), p)

    def tiles_of(i):
        rows = slice(i * 256, (i + 1) * 256)
        return (
            decode(low[rows, :], low_scale).reshape(BS, BS, 128),
            decode(high[rows, :], high_scale).reshape(BS, BS, 128),
        )

    strips = [
        with_row(
            decode(low[1024:1280, :], low_scale), BS - 1, s2 * both(hleft, hright, slice(560, 576))
        ),
        with_row(
            both(left, right, slice(0, 256)), 0, has_low * decode(low[1280:1296, :], low_scale)
        ),
        with_row(
            both(left, right, slice(256, 512)),
            BS - 1,
            has_high * decode(high[1280:1296, :], high_scale),
        ),
        with_row(
            decode(high[1024:1280, :], high_scale), 0, s2 * both(hleft, hright, slice(576, 592))
        ),
    ]
    pull_all(4, tiles_of, strips, weights, pulled)
    for block in range(4):
        xs = slice(block * BS, (block + 1) * BS)
        plan_masks(p * 4 + block, p * 4, turned, mask.at[block], range(8, 12))
        total = collect(p * 4 + block, p * 4, pulled, mask.at[block], range(8, 12))
        if p == 0:
            scale = scale_of(earlier, 2048)
            passed = decode(earlier[block * 512 : (block + 1) * 512, :], scale)
            passed = passed.reshape(BS, 2 * BS, 128)
        for half in range(2):
            zs = slice(half * BS, (half + 1) * BS)
            cells = total[:, half * 128 : (half + 1) * 128].reshape(BS, BS, 128)
            cells = cells + partial[xs, zs, :]
            if p == 0:
                cells = cells - passed[:, zs]
            out[0, xs, zs, :] = cells


PARAMS = pltpu.CompilerParams(vmem_limit_bytes=24 * 1024 * 1024)


def shape(dims, dtype):
    return jax.ShapeDtypeStruct(dims, dtype)


def call(kernel, out_shape, args, scratch=(), stencil=None, **more):
    specs = [
        pl.BlockSpec(memory_space=pltpu.SMEM if k == stencil else pltpu.VMEM)
        for k in range(len(args))
    ]
    more.setdefault("in_specs", specs)
    more.setdefault("compiler_params", PARAMS)
    return pl.pallas_call(kernel, out_shape=out_shape, scratch_shapes=list(scratch), **more)(*args)


def body(volume, shift_code, frac_code, stencil):
    z_count = lax.axis_size("gz")
    y_count = lax.axis_size("gy")
    strip = shape((512, 128), BF16)
    cube = shape(volume.shape[1:], F32)
    mate, far = call(
        pack_kernel,
        (strip, strip),
        (volume,),
    )
    far = swap(far, True)
    mate = swap(mate, False)
    slab = shape((1280, 128), BF16)
    down0, up0, down1, up1, first, sides = call(
        slab_kernel,
        (slab,) * 4 + (shape(volume.shape[1:], BF16), shape((2, 2, 256, 128), BF16)),
        (volume, mate, far),
    )
    highs = [ring(down0, "gz", -1)]
    lows = [ring(up0, "gz", 1)]
    highs.append(ring(down1, "gz", -1))
    lows.append(ring(up1, "gz", 1))
    following = ring(first, "phase", -1)
    gathered, keys, weights, codes = call(
        functools.partial(near_kernel, z_count, y_count),
        (
            shape((8, 256, 256), BF16),
            shape((4, 8, 256), I32),
            shape((3, 8, 256), F32),
            shape((BS, 128), BF16),
        ),
        (volume, sides, shift_code, frac_code),
        [
            pltpu.VMEM((8, 256), F32),
            pltpu.VMEM((8, 256), F32),
            pltpu.VMEM((8, 1024, 256), BF16),
        ],
    )
    mask_in, weights_in = call(
        functools.partial(plan_kernel, z_count, y_count),
        (shape((8, 768, 256), BF16), shape((3, BS, 128), F32)),
        (codes,),
        [
            pltpu.VMEM((BS, 128), F32),
            pltpu.VMEM((BS, 128), F32),
            pltpu.VMEM((BS, 128, 128), I16),
        ],
    )
    scratch = [
        pltpu.VMEM((4, 1024, 256), BF16),
        pltpu.VMEM(volume.shape[1:], F32),
        pltpu.VMEM((2, 4, 256, 128), BF16),
    ]
    face = shape((64, 128), BF16)
    peak = shape((32, 128), F32)
    packed = shape((2, 256, 256), BF16)
    message = shape((592, 128), BF16)
    smoothed0, face00, face10, peak0, packed_res, packed_smoothed = call(
        functools.partial(forward_kernel, 0),
        (cube, face, face, peak, packed, packed),
        (volume[1], lows[0], highs[0], gathered[:4], keys, weights, stencil, weights_in),
        scratch,
        stencil=6,
    )
    smoothed1, face01, face11, peak1, mate, far, res_left, res_right = call(
        functools.partial(forward_kernel, 1),
        (cube, face, face, peak, message, message, strip, strip),
        (
            following, lows[1], highs[1], gathered[4:], keys, weights, stencil,
            packed_res, packed_smoothed, codes,
        ),
        scratch,
        stencil=6,
    )
    far = swap(far, True)
    mate = swap(mate, False)
    fhigh = ring(jnp.concatenate([face00, face01]), "gz", -1)
    flow = ring(jnp.concatenate([face10, face11]), "gz", 1)
    hleft, hright, left, right, sides, parity, tops = call(
        functools.partial(join_kernel, y_count),
        (
            message, message, strip, strip,
            shape((2, 2, 272, 128), F32), shape((2, 32, 128), F32), shape((8, 128), F32),
        ),
        (mate, far, res_left, res_right, peak0, peak1, stencil),
        stencil=6,
    )
    slab = shape((1344, 128), I16)
    common = (flow, fhigh, sides, parity, tops, codes, hleft, hright, stencil)
    smoothed1, down1, up1, ahead = call(
        functools.partial(complete_kernel, 1, z_count),
        (cube, slab, slab, shape((2064, 128), I16)),
        (smoothed1, *common),
        stencil=9,
    )
    high1 = ring(down1, "gz", -1)
    low1 = ring(up1, "gz", 1)
    earlier = ring(ahead, "phase", 1)
    smoothed0, down0, up0 = call(
        functools.partial(complete_kernel, 0, z_count),
        (cube, slab, slab),
        (smoothed0, *common),
        stencil=9,
    )
    high0 = ring(down0, "gz", -1)
    low0 = ring(up0, "gz", 1)

    def scratch_of(rows, tiles, width):
        return [
            pltpu.VMEM((BS, 128), F32),
            pltpu.VMEM((BS, 128), F32),
            pltpu.VMEM((3, BS, 128), F32),
            pltpu.VMEM((BS, 128, 128), I16),
            pltpu.VMEM((rows, 512, 128), BF16),
            pltpu.VMEM((tiles, width, 256), BF16),
        ]

    partial0, partial1 = call(
        inner_kernel,
        (cube, cube),
        (smoothed0, smoothed1, mask_in, weights_in),
        [pltpu.VMEM((16, 512, 128), BF16)],
    )
    vmem = pl.BlockSpec(memory_space=pltpu.VMEM)
    smem = pl.BlockSpec(memory_space=pltpu.SMEM)
    anywhere = pl.BlockSpec(memory_space=pl.ANY)
    out = ()
    for p, partial, low, high in ((1, partial1, low1, high1), (0, partial0, low0, high0)):
        more = () if p == 1 else (earlier, out)
        out = call(
            functools.partial(outer_kernel, p, z_count, y_count),
            shape(volume.shape, F32),
            (partial, low, high, hleft, hright, left, right, stencil, *more),
            scratch_of(12, 4, 1280),
            grid=(1,),
            in_specs=[vmem] * 7 + [smem] + ([vmem, anywhere] if more else []),
            out_specs=pl.BlockSpec((1,) + volume.shape[1:], functools.partial(phase_block, p)),
            input_output_aliases={9: 0} if more else {},
        )
    return out


def phase_block(p, step):
    return p, 0, 0, 0


def solution(mesh):
    placed = (
        P("phase", None, "gz", "gy"),
        P("phase", "gz", "gy", None),
        P("phase", "gz", "gy", None),
        P(),
    )
    return jax.shard_map(
        body, mesh=mesh, in_specs=placed, out_specs=P("phase", None, "gz", "gy"), check_vma=False
    )
```

```python
import functools

import jax
import jax.numpy as jnp
from jax import lax
from jax.experimental import pallas as pl
from jax.experimental.pallas import tpu as pltpu
from jax.sharding import PartitionSpec as P

BS = 16
F32 = jnp.float32
BF16 = jnp.bfloat16
I32 = jnp.int32
I16 = jnp.int16
NONE = -4096


def iota(shape, dim, dtype=I32):
    return lax.broadcasted_iota(dtype, shape, dim)


def ring(cells, axis, by):
    count = lax.axis_size(axis)
    return lax.ppermute(cells, axis, [(i, (i + by) % count) for i in range(count)])


def onehot(hit):
    return jnp.where(hit, jnp.array(1, BF16), jnp.array(0, BF16))


def dot(left, right):
    return jnp.dot(left, right, preferred_element_type=F32)


def swap(cells, far):
    count = lax.axis_size("gy")
    step = -1 if far else 1
    pairs = [(i, (i + (step if i % 2 == 0 else -step)) % count) for i in range(count)]
    return lax.ppermute(cells, "gy", pairs)


def by_parity(first, second):
    return jnp.where(lax.axis_index("gy") % 2 == 1, first, second)


def spread_matrix():
    return onehot(iota((128, 2048), 0, I16) == (iota((1, 2048), 1) >> 4).astype(I16))


def strip_matrix():
    column = iota((1, 256), 1)
    right = column >> 7
    group = ((column & 127) >> 4) ^ (4 - 4 * right)
    wanted = group * 128 + (column & 15) + right * 112
    return onehot(iota((1024, 256), 0, I16) == wanted.astype(I16))


def displacements(codes):
    dx = (codes * 57) >> 9
    rest = codes - 9 * dx
    dz = (rest * 11) >> 5
    dy = rest - 3 * dz
    return dx - 1, dz - 1, dy - 1


def fraction(level):
    return (level + 1).astype(F32) / 5.0


def encode(values, inverse):
    share = values * inverse
    root = share * lax.rsqrt(jnp.abs(share) + 1e-30)
    return ((root * 32767.0 + 12582912.0) - 12582912.0).astype(I32).astype(I16)


def decode(coded, scale):
    count = coded.astype(F32)
    return count * jnp.abs(count) * (scale * (1.0 / (32767.0 * 32767.0)))


def scale_of(message, row):
    return jnp.exp2(message[row : row + 16, :].astype(F32)[2:3])


def pack_kernel(vol, mate, far):
    for h in range(2):
        tiles = [
            vol[i // 4, (i % 4) * BS : (i % 4 + 1) * BS, h * BS : (h + 1) * BS].reshape(256, 128)
            for i in range(8)
        ]
        strips = dot(jnp.concatenate(tiles, axis=1), strip_matrix())
        rows = slice(h * 256, (h + 1) * 256)
        left, right = strips[:, :128], strips[:, 128:]
        mate[rows, :] = by_parity(left, right).astype(BF16)
        far[rows, :] = by_parity(right, left).astype(BF16)


def pack_strips(tiles, p):
    chosen = strip_matrix()[p * 512 : (p + 1) * 512]
    return [dot(jnp.concatenate(half, axis=1), chosen) for half in tiles]


def mixed(first, second, p):
    low = iota(first.shape, first.ndim - 1) < 64
    return jnp.where(low, first, second) if p == 0 else jnp.where(low, second, first)


def slab_kernel(vol, mate, far, *outs):
    first, sides = outs[4:]
    first[...] = vol[0]
    for half in range(2):
        rows = slice(half * 256, (half + 1) * 256)
        theirs = [mate[rows, :].astype(F32), far[rows, :].astype(F32)]
        hleft, hright = by_parity(*theirs), by_parity(*theirs[::-1])
        for p in range(2):
            out = outs[p * 2 + half]
            cells = vol[p, :, half * BS : (half + 1) * BS, :]
            out[0:1024, :] = cells.reshape(1024, 128)
            cells = mixed(hleft, hright, p).astype(BF16)
            out[1024:1280, :] = cells
            sides[p, half] = cells


def near_kernel(
    z_count, y_count, vol, sides, shift, frac,
    gathered, keys, weights, codes, shifts, fracs, mask,
):
    rz = lax.axis_index("gz")
    ry = lax.axis_index("gy")
    both = [
        jnp.concatenate([part[0, 0].astype(F32), part[1, 0].astype(F32)], axis=1)
        for part in (shift, frac)
    ]
    at = iota((BS, 128), 0)
    codes[...] = jnp.where(at == 0, both[0], jnp.where(at == 1, both[1], 0.0)).astype(BF16)
    spread = dot(codes[...], spread_matrix())
    for i in range(8):
        shifts[i : i + 1, :] = spread[0:1, i * 256 : (i + 1) * 256]
        fracs[i : i + 1, :] = spread[1:2, i * 256 : (i + 1) * 256]
    dx, dz, dy = displacements(shifts[...].astype(I32))
    row = iota((8, 256), 0)
    lane = iota((8, 256), 1)
    bz = lane >> 7
    by = (lane >> 4) & 7
    yy = lane & 15
    bx = row & 3
    source_x = jnp.clip(bx + dx, 0, 3)
    source_z = jnp.clip(rz * 2 + bz + dz, 0, 2 * z_count - 1) - rz * 2 + 1
    source_y = jnp.clip(ry * 8 + by + dy, 0, 8 * y_count - 1) - ry * 8
    inside = (source_y >= 0) & (source_y < 8)
    keys[0] = jnp.where(inside, (source_x - bx + 1) * 4 + source_z, -1)
    keys[1] = source_y * BS + yy
    keys[2] = jnp.where(inside, -1, source_z)
    keys[3] = (jnp.where(source_y < 0, row >> 2, 1 - (row >> 2)) * 4 + source_x) * BS + yy
    levels = fracs[...].astype(I32)
    weights[0] = fraction(levels >> 4)
    weights[1] = fraction((levels >> 2) & 3)
    weights[2] = jnp.where(yy == 15, 0.0, fraction(levels & 3))

    def step(block):
        for p in range(2):

            def tile(xb, zb):
                xs = slice(xb * BS, (xb + 1) * BS)
                return vol[p, xs, (zb - 1) * BS : zb * BS, :].reshape(256, 128)

            i = p * 4 + block
            strips = [sides[p, 0], sides[p, 1]]
            gathered[i] = gather(i, keys, mask.at[i], tile, strips, (1, 2)).astype(BF16)

    for block in range(4):
        step(block)


def gather(i, keys, mask, tile, strips, z_blocks):
    here = [keys[k, i : i + 1, :] for k in range(4)]
    sublane = iota((128, 256), 0, I16)
    pieces = []

    def add(piece, hit, place):
        at = len(pieces) * 128
        mask[at : at + 128, :] = onehot(sublane == jnp.where(hit, place, NONE).astype(I16))
        pieces.append(piece)

    for d in range(3):
        xb = i % 4 + d - 1
        if not 0 <= xb < 4:
            continue
        for zb in z_blocks:
            add(tile(xb, zb), here[0] == d * 4 + zb, here[1])
    for k, zb in enumerate(z_blocks):
        add(strips[k], here[2] == zb, here[3])
    return dot(jnp.concatenate(pieces, axis=1), mask[0 : len(pieces) * 128, :])


def forward_kernel(p, coming, low, high, partial, keys, weights, stencil, *rest):
    if p == 0:
        _, *rest = rest
    if p == 1:
        before_res, before_smoothed, codes, *rest = rest
        smoothed, face0, face1, peak, mate, far, res_left, res_right, mask, res, strips_in = rest
    else:
        smoothed, face0, face1, peak, packed_res, packed_smoothed, mask, res, strips_in = rest
    s0, s1, s2, s3 = (stencil[k] for k in range(4))
    last_z = iota((1, BS, 128), 1) == BS - 1

    for block in range(4):
        xs = slice(block * BS, (block + 1) * BS)
        i = p * 4 + block

        def tile(xb, zb):
            return (low if zb == 0 else high)[xb * 256 : (xb + 1) * 256, :]

        strips = [slab[1024:1280, :] for slab in (low, high)]
        more = gather(i, keys, mask.at[block], tile, strips, (0, 3))
        gathered = partial[block].astype(F32) + more
        levels_here = [weights[k, i : i + 1, :] for k in range(3)]
        for half in range(2):
            part = slice(half * 128, (half + 1) * 128)
            zs = slice(half * BS, (half + 1) * BS)
            wx, wz, wy = (w[:, part].reshape(1, 1, 128) for w in levels_here)
            wz = jnp.where(last_z, 0.0, wz)
            cells = gathered[:, part].reshape(BS, BS, 128)
            cells = cells + wy * (pltpu.roll(cells, 127, 2) - cells)
            cells = cells + wz * (pltpu.roll(cells, BS - 1, 1) - cells)
            after = jnp.concatenate([cells[1:], cells[BS - 1 :]], axis=0)
            cells = cells + wx * (after - cells)
            cells = cells - coming[xs, zs, :].astype(F32)
            res[xs, zs, :] = cells
            strips_in[half, block] = cells.astype(BF16).reshape(256, 128)
            if half == 0:
                face0[xs, :] = cells[:, 0, :].astype(BF16)
            else:
                face1[xs, :] = cells[:, BS - 1, :].astype(BF16)

    packed = pack_strips([[strips_in[half, k] for k in range(4)] for half in range(2)], p)
    if p == 0:
        for half in range(2):
            packed_res[half] = packed[half].astype(BF16)
    else:
        messages = []
        group = iota((BS, 128), 1) & 15
        packed = [packed[half] + before_res[half].astype(F32) for half in range(2)]
        for side, edge, out in ((0, 0, res_left), (1, 15, res_right)):
            columns, edges = [], []
            for half in range(2):
                flat = packed[half][:, side * 128 : (side + 1) * 128]
                out[half * 256 : (half + 1) * 256, :] = flat.astype(BF16)
                cells = flat.reshape(BS, BS, 128)
                column = jnp.zeros((BS, 128), F32)
                for xi in range(BS):
                    turn = (xi - edge + 64 - 64 * side) % 128
                    plane = pltpu.roll(cells[xi], turn, 1) if turn else cells[xi]
                    column = jnp.where(group == xi, plane, column)
                columns.append(column)
                edges.append(cells[:, half * (BS - 1), :])
            messages.append(jnp.concatenate([codes[...].astype(F32)] + columns + edges, axis=0))
        mate[512:592, :] = by_parity(*messages).astype(BF16)
        far[512:592, :] = by_parity(*messages[::-1]).astype(BF16)

    zi = iota((32, 128), 0)
    lane = iota((32, 128), 1)

    def smooth(block, top):
        x0 = block * BS
        before = res[x0 - 1] if block else jnp.zeros((32, 128), F32)
        cells = res[x0]
        for xi in range(BS):
            if xi < BS - 1:
                after = res[x0 + xi + 1]
            else:
                after = res[x0 + BS] if block < 3 else jnp.zeros((32, 128), F32)
            top = jnp.maximum(top, jnp.abs(cells))
            z_low = jnp.where(zi == 0, 0.0, pltpu.roll(cells, 1, 0))
            z_high = jnp.where(zi == 31, 0.0, pltpu.roll(cells, 31, 0))
            y_low = jnp.where(lane == 0, 0.0, pltpu.roll(cells, 1, 1))
            y_high = jnp.where(lane == 127, 0.0, pltpu.roll(cells, 127, 1))
            value = s0 * cells + s1 * (before + after)
            value = value + s2 * (z_low + z_high) + s3 * (y_low + y_high)
            smoothed[x0 + xi] = value
            rounded = value.astype(BF16)
            rows = pl.ds(xi * BS, BS)
            strips_in[0, block, rows, :] = rounded[:BS]
            strips_in[1, block, rows, :] = rounded[BS:]
            before = cells
            cells = after
        return top

    top = jnp.zeros((32, 128), F32)
    for block in range(4):
        top = smooth(block, top)
    peak[...] = top
    packed = pack_strips([[strips_in[half, k] for k in range(4)] for half in range(2)], p)
    for half in range(2):
        if p == 0:
            packed_smoothed[half] = packed[half].astype(BF16)
        else:
            rows = slice(half * 256, (half + 1) * 256)
            cells = packed[half] + before_smoothed[half].astype(F32)
            mate[rows, :] = by_parity(cells[:, :128], cells[:, 128:]).astype(BF16)
            far[rows, :] = by_parity(cells[:, 128:], cells[:, :128]).astype(BF16)


def join_kernel(
    y_count, mate, far, res_left, res_right, peak0, peak1, stencil,
    hleft, hright, left, right, sides, parity, tops,
):
    ry = lax.axis_index("gy")
    s3 = stencil[3]
    theirs = [mate[...].astype(F32), far[...].astype(F32)]
    messages = [by_parity(*theirs), by_parity(*theirs[::-1])]
    hleft[...] = messages[0].astype(BF16)
    hright[...] = messages[1].astype(BF16)
    columns = [
        messages[0][528:560] * (ry > 0).astype(F32),
        messages[1][528:560] * (ry < y_count - 1).astype(F32),
    ]
    turned = pltpu.roll(columns[1], 127, 1)
    lane = iota((32, 128), 1)
    for odd in range(2):
        parity[odd] = s3 * jnp.where((lane & 1) == odd, columns[0], turned)
    group = iota((256, 128), 1) & 15
    strips = []
    for out, message, own, edge in (
        (left, messages[0], res_left, 15), (right, messages[1], res_right, 0)
    ):
        for half in range(2):
            rows = slice(half * 256, (half + 1) * 256)
            beside = pltpu.roll(own[rows, :].astype(F32), 79 if edge else 49, 1)
            cells = message[rows] + jnp.where(group == edge, s3 * beside, 0.0)
            out[rows, :] = cells.astype(BF16)
            strips.append(cells)
    inner = jnp.maximum(jnp.max(peak0[...]), jnp.max(peak1[...]))
    for cells in columns:
        inner = jnp.maximum(inner, jnp.max(jnp.abs(cells)))
    edges = [message[560:592] for message in messages]
    direct = jnp.array(1e-30, F32)
    for cells in (*strips, *edges):
        direct = jnp.maximum(direct, jnp.max(jnp.abs(cells)))
    tops[...] = jnp.where(iota((8, 128), 0) == 0, inner, direct)
    for half in range(2):
        part = slice(half * BS, (half + 1) * BS)
        for p in range(2):
            sides[p, half, 0:256, :] = mixed(strips[half], strips[2 + half], p)
            sides[p, half, 256:272, :] = mixed(edges[0][part], edges[1][part], p)


def power_of(z_count, tops, flow, fhigh, stencil):
    rz = lax.axis_index("gz")
    low = jnp.max(jnp.abs(flow[...].astype(F32))) * (rz > 0).astype(F32)
    high = jnp.max(jnp.abs(fhigh[...].astype(F32))) * (rz < z_count - 1).astype(F32)
    inner = jnp.maximum(tops[0:1, :], jnp.maximum(low, high))
    top = inner * (stencil[0] + 2.0 * (stencil[1] + stencil[2] + stencil[3]))
    top = jnp.maximum(top, tops[1:2, :])
    return jnp.ceil(jnp.log(top) * 1.4426950408889634)


def complete_kernel(
    p, z_count, partial, flow, fhigh, sides, parity, tops, codes, hleft, hright, stencil, *rest
):
    smoothed, down, up, *ahead = rest
    rz = lax.axis_index("gz")
    has_low = (rz > 0).astype(F32) * stencil[2]
    has_high = (rz < z_count - 1).astype(F32) * stencil[2]
    power = power_of(z_count, tops, flow, fhigh, stencil)
    inverse = 1.0 / jnp.exp2(power)
    tail = jnp.where(iota((BS, 128), 0) == 2, power, codes[...].astype(F32))
    tail = [tail] + [message[512:528, :].astype(F32) for message in (hleft, hright)]
    tail = jnp.concatenate(tail, axis=0).astype(I32).astype(I16)
    for half, out in enumerate((down, up)):
        out[1024:1296, :] = encode(sides[p, half], inverse)
        out[1296:1344, :] = tail
    for out in ahead:
        out[2048:2064, :] = tail[0:BS]
    lane = iota((32, 128), 1)
    at_edge = (lane == 0) | (lane == 127)
    zi = iota((BS, 128), 0)
    low_edge = zi == 0
    high_edge = zi == BS - 1

    def step(block):
        i = p * 4 + block
        turn = (128 - i * BS) % 128
        sides_here = [pltpu.roll(parity[odd], turn, 1) for odd in range(2)]
        rows = slice(i * BS, (i + 1) * BS)
        lows = flow[rows, :].astype(F32) * has_low
        highs = fhigh[rows, :].astype(F32) * has_high
        for xi in range(BS):
            side = sides_here[xi & 1]
            if xi:
                side = pltpu.roll(side, 128 - xi, 1)
            x = block * BS + xi
            value = partial[x] + jnp.where(at_edge, side, 0.0)
            first = value[:BS] + jnp.where(low_edge, lows[xi : xi + 1], 0.0)
            second = value[BS:] + jnp.where(high_edge, highs[xi : xi + 1], 0.0)
            smoothed[x, 0:BS, :] = first
            smoothed[x, BS : 2 * BS, :] = second
            first = encode(first, inverse)
            second = encode(second, inverse)
            out_rows = slice(x * BS, (x + 1) * BS)
            down[out_rows, :] = first
            up[out_rows, :] = second
            for out in ahead:
                out[x * 32 : x * 32 + BS, :] = first
                out[x * 32 + BS : x * 32 + 2 * BS, :] = second

    for block in range(4):
        step(block)


def turned_warp(cells, wx, wy, wz):
    scaled = wy * cells
    cells = cells - scaled + pltpu.roll(scaled, 1, 2)
    scaled = wz * cells
    cells = cells - scaled + pltpu.roll(scaled, 1, 1)
    scaled = wx * cells[: BS - 1]
    zero = jnp.zeros((1, BS, 128), F32)
    cells = cells - jnp.concatenate([scaled, zero], axis=0) + jnp.concatenate([zero, scaled], axis=0)
    cells = cells.reshape(256, 128)
    high = cells.astype(BF16)
    return high, (cells - high.astype(F32)).astype(BF16)


def targets(z_count, y_count, shifts, fracs, p, turned, weights):
    rz = lax.axis_index("gz")
    ry = lax.axis_index("gy")
    dx, dz, dy = displacements(shifts[...].astype(I32))
    row = iota((BS, 128), 0)
    lane = iota((BS, 128), 1)
    yy = lane & 15
    if p is None:
        number, zb, by, count = row >> 1, 1 + (row & 1), lane >> 4, 16
    else:
        strip = row >= 8
        zb = jnp.where(strip, row & 3, 3 * (row & 1))
        number = p * 4 + jnp.where(strip, (lane >> 4) & 3, (row >> 1) & 3)
        from_left = (lane < 64) if p == 0 else (lane >= 64)
        by = jnp.where(strip, jnp.where(from_left, -1, 8), lane >> 4)
        count = 12
    bx = number & 3
    dest_z = rz * 2 + zb - 1
    dest_y = ry * 8 + by
    there = (dest_z >= 0) & (dest_z < 2 * z_count) & (dest_y >= 0) & (dest_y < 8 * y_count)
    source_x = jnp.clip(bx + dx, 0, 3)
    source_z = jnp.clip(dest_z + dz, 0, 2 * z_count - 1) - rz * 2
    source_y = jnp.clip(dest_y + dy, 0, 8 * y_count - 1) - ry * 8
    there = there & (source_z >= 0) & (source_z < 2) & (source_y >= 0) & (source_y < 8)
    target = ((number >> 2) * 4 + source_x) * 256 + source_z * 128 + source_y * BS + yy
    target = jnp.where(there, target, NONE).astype(F32)
    nobody = jnp.full((112, 128), float(NONE), F32)
    columns = jnp.concatenate([target, nobody], axis=0).T
    for r in range(count):
        turned[r] = jnp.broadcast_to(columns[:, r : r + 1], (128, 128)).astype(I16)
    levels = fracs[...].astype(I32)
    weights[0] = fraction(levels >> 4)
    weights[1] = fraction((levels >> 2) & 3)
    weights[2] = jnp.where(yy == 15, 0.0, fraction(levels & 3))


def strip_codes(p, zb, sources, half, shifts, fracs):
    lane = iota((1, 128), 1)
    picked = []
    for source, edge in zip(sources, (7, 0)):
        block = p * 64 + (((lane >> 4) & 3) * 2 + half) * 8 + edge
        hit = iota((128, 128), 0, I16) == block.astype(I16)
        picked.append(dot(source, onehot(hit)))
    cells = mixed(*picked, p)
    shifts[8 + zb : 9 + zb, :] = cells[0:1, :]
    fracs[8 + zb : 9 + zb, :] = cells[1:2, :]


def pull_all(count, tiles_of, strips, weights, pulled):
    last_z = iota((1, BS, 128), 1) == BS - 1

    def put(r, cells):
        wx, wz, wy = (weights[k, r : r + 1, :].reshape(1, 1, 128) for k in range(3))
        first, second = turned_warp(cells, wx, wy, jnp.where(last_z, 0.0, wz))
        pulled[r, 0:256, :] = first
        pulled[r, 256:512, :] = second

    for k, cells in enumerate(strips):
        put(count * 2 + k, cells)
    for i in range(count):
        for k, cells in enumerate(tiles_of(i)):
            put(i * 2 + k, cells)


def tiles_for(i, base, strips):
    near = [d for d in (-1, 0, 1) if 0 <= i % 4 + d < 4]
    return [(i - base + d) * 2 + k for d in near for k in range(2)] + list(strips)


def plan_masks(i, base, turned, mask, strips):
    lanes = iota((128, 256), 1, I16) + jnp.array(i * 256, I16)
    for at, r in enumerate(tiles_for(i, base, strips)):
        rows = slice(at * 128, (at + 1) * 128)
        lower = len(strips) > 0 and (r == 8 or (r < 8 and r % 2 == 0))
        upper = len(strips) > 0 and (r == 11 or (r < 8 and r % 2 == 1))
        for half, skipped in ((0, upper), (1, lower)):
            part = slice(half * 128, (half + 1) * 128)
            if skipped:
                mask[rows, part] = jnp.zeros((128, 128), BF16)
            else:
                mask[rows, part] = onehot(turned[r] == lanes[:, part])


def collect(i, base, pulled, mask, strips):
    rows = tiles_for(i, base, strips)
    pieces = jnp.concatenate([pulled[r] for r in rows], axis=1)
    both = dot(pieces, mask[0 : len(rows) * 128, :])
    return both[0:256] + both[256:512]


def plan_kernel(z_count, y_count, codes, mask, weights, shifts, fracs, turned):
    own = dot(codes[...], spread_matrix())
    for i in range(8):
        for half in range(2):
            part = slice(i * 256 + half * 128, i * 256 + half * 128 + 128)
            shifts[i * 2 + half : i * 2 + half + 1, :] = own[0:1, part]
            fracs[i * 2 + half : i * 2 + half + 1, :] = own[1:2, part]
    targets(z_count, y_count, shifts, fracs, None, turned, weights)
    for i in range(8):
        plan_masks(i, 0, turned, mask.at[i], ())


def inner_kernel(smoothed0, smoothed1, mask, weights, out0, out1, pulled):
    for p, smoothed in enumerate((smoothed0, smoothed1)):

        def tiles_of(i):
            xs = slice(i * BS, (i + 1) * BS)
            return smoothed[xs, 0:BS, :], smoothed[xs, BS : 2 * BS, :]

        pull_all(4, tiles_of, (), weights.at[:, p * 8 : p * 8 + 8], pulled.at[p * 8 : p * 8 + 8])
    for i in range(8):
        p, block = divmod(i, 4)
        xs = slice(block * BS, (block + 1) * BS)
        total = collect(i, 0, pulled, mask.at[i], ())
        for half in range(2):
            zs = slice(half * BS, (half + 1) * BS)
            cells = total[:, half * 128 : (half + 1) * 128].reshape(BS, BS, 128)
            if p == 0:
                out0[xs, zs, :] = cells
            else:
                out1[xs, zs, :] = cells - smoothed0[xs, zs, :]


def outer_kernel(
    p, z_count, y_count, partial, low, high, hleft, hright, left, right, stencil, *rest
):
    if p == 0:
        earlier, _, *rest = rest
    out, shifts, fracs, weights, turned, pulled, mask = rest
    rz = lax.axis_index("gz")
    s2 = stencil[2]
    has_low = (rz > 0).astype(F32) * s2
    has_high = (rz < z_count - 1).astype(F32) * s2
    shifts[...] = jnp.zeros((BS, 128), F32)
    fracs[...] = jnp.zeros((BS, 128), F32)
    spread = spread_matrix()[:, p * 1024 : (p + 1) * 1024]
    tails = [
        [slab[1296 + k * BS : 1312 + k * BS, :].astype(F32).astype(BF16) for k in range(3)]
        for slab in (low, high)
    ]
    for k, half in ((0, 1), (1, 0)):
        theirs = dot(tails[k][0], spread)
        for i in range(4):
            part = slice(i * 256 + half * 128, i * 256 + half * 128 + 128)
            shifts[i * 2 + k : i * 2 + k + 1, :] = theirs[0:1, part]
            fracs[i * 2 + k : i * 2 + k + 1, :] = theirs[1:2, part]
    beside = (hleft[512:528, :], hright[512:528, :])
    strip_codes(p, 0, tails[0][1:], 1, shifts, fracs)
    strip_codes(p, 1, beside, 0, shifts, fracs)
    strip_codes(p, 2, beside, 1, shifts, fracs)
    strip_codes(p, 3, tails[1][1:], 0, shifts, fracs)
    targets(z_count, y_count, shifts, fracs, p, turned, weights)
    low_scale = scale_of(low, 1296)
    high_scale = scale_of(high, 1296)
    zi = iota((1, BS, 128), 1)

    def with_row(cells, row, values):
        cells = cells.reshape(BS, BS, 128)
        return cells + jnp.where(zi == row, values.reshape(BS, 1, 128), 0.0)

    def both(first, second, rows):
        return mixed(first[rows, :].astype(F32), second[rows, :].astype(F32), p)

    def tiles_of(i):
        rows = slice(i * 256, (i + 1) * 256)
        return (
            decode(low[rows, :], low_scale).reshape(BS, BS, 128),
            decode(high[rows, :], high_scale).reshape(BS, BS, 128),
        )

    strips = [
        with_row(
            decode(low[1024:1280, :], low_scale), BS - 1, s2 * both(hleft, hright, slice(560, 576))
        ),
        with_row(
            both(left, right, slice(0, 256)), 0, has_low * decode(low[1280:1296, :], low_scale)
        ),
        with_row(
            both(left, right, slice(256, 512)),
            BS - 1,
            has_high * decode(high[1280:1296, :], high_scale),
        ),
        with_row(
            decode(high[1024:1280, :], high_scale), 0, s2 * both(hleft, hright, slice(576, 592))
        ),
    ]
    pull_all(4, tiles_of, strips, weights, pulled)
    for block in range(4):
        xs = slice(block * BS, (block + 1) * BS)
        plan_masks(p * 4 + block, p * 4, turned, mask.at[block], range(8, 12))
        total = collect(p * 4 + block, p * 4, pulled, mask.at[block], range(8, 12))
        if p == 0:
            scale = scale_of(earlier, 2048)
            passed = decode(earlier[block * 512 : (block + 1) * 512, :], scale)
            passed = passed.reshape(BS, 2 * BS, 128)
        for half in range(2):
            zs = slice(half * BS, (half + 1) * BS)
            cells = total[:, half * 128 : (half + 1) * 128].reshape(BS, BS, 128)
            cells = cells + partial[xs, zs, :]
            if p == 0:
                cells = cells - passed[:, zs]
            out[0, xs, zs, :] = cells


PARAMS = pltpu.CompilerParams(vmem_limit_bytes=24 * 1024 * 1024)


def shape(dims, dtype):
    return jax.ShapeDtypeStruct(dims, dtype)


def call(kernel, out_shape, args, scratch=(), stencil=None, **more):
    specs = [
        pl.BlockSpec(memory_space=pltpu.SMEM if k == stencil else pltpu.VMEM)
        for k in range(len(args))
    ]
    more.setdefault("in_specs", specs)
    more.setdefault("compiler_params", PARAMS)
    return pl.pallas_call(kernel, out_shape=out_shape, scratch_shapes=list(scratch), **more)(*args)


def body(volume, shift_code, frac_code, stencil):
    z_count = lax.axis_size("gz")
    y_count = lax.axis_size("gy")
    strip = shape((512, 128), BF16)
    cube = shape(volume.shape[1:], F32)
    mate, far = call(
        pack_kernel,
        (strip, strip),
        (volume,),
    )
    far = swap(far, True)
    mate = swap(mate, False)
    slab = shape((1280, 128), BF16)
    down0, up0, down1, up1, first, sides = call(
        slab_kernel,
        (slab,) * 4 + (shape(volume.shape[1:], BF16), shape((2, 2, 256, 128), BF16)),
        (volume, mate, far),
    )
    highs = [ring(down0, "gz", -1)]
    lows = [ring(up0, "gz", 1)]
    highs.append(ring(down1, "gz", -1))
    lows.append(ring(up1, "gz", 1))
    following = ring(first, "phase", -1)
    gathered, keys, weights, codes = call(
        functools.partial(near_kernel, z_count, y_count),
        (
            shape((8, 256, 256), BF16),
            shape((4, 8, 256), I32),
            shape((3, 8, 256), F32),
            shape((BS, 128), BF16),
        ),
        (volume, sides, shift_code, frac_code),
        [
            pltpu.VMEM((8, 256), F32),
            pltpu.VMEM((8, 256), F32),
            pltpu.VMEM((8, 1024, 256), BF16),
        ],
    )
    mask_in, weights_in = call(
        functools.partial(plan_kernel, z_count, y_count),
        (shape((8, 768, 256), BF16), shape((3, BS, 128), F32)),
        (codes,),
        [
            pltpu.VMEM((BS, 128), F32),
            pltpu.VMEM((BS, 128), F32),
            pltpu.VMEM((BS, 128, 128), I16),
        ],
    )
    scratch = [
        pltpu.VMEM((4, 1024, 256), BF16),
        pltpu.VMEM(volume.shape[1:], F32),
        pltpu.VMEM((2, 4, 256, 128), BF16),
    ]
    face = shape((64, 128), BF16)
    peak = shape((32, 128), F32)
    packed = shape((2, 256, 256), BF16)
    message = shape((592, 128), BF16)
    smoothed0, face00, face10, peak0, packed_res, packed_smoothed = call(
        functools.partial(forward_kernel, 0),
        (cube, face, face, peak, packed, packed),
        (volume[1], lows[0], highs[0], gathered[:4], keys, weights, stencil, weights_in),
        scratch,
        stencil=6,
    )
    smoothed1, face01, face11, peak1, mate, far, res_left, res_right = call(
        functools.partial(forward_kernel, 1),
        (cube, face, face, peak, message, message, strip, strip),
        (
            following, lows[1], highs[1], gathered[4:], keys, weights, stencil,
            packed_res, packed_smoothed, codes,
        ),
        scratch,
        stencil=6,
    )
    far = swap(far, True)
    mate = swap(mate, False)
    fhigh = ring(jnp.concatenate([face00, face01]), "gz", -1)
    flow = ring(jnp.concatenate([face10, face11]), "gz", 1)
    hleft, hright, left, right, sides, parity, tops = call(
        functools.partial(join_kernel, y_count),
        (
            message, message, strip, strip,
            shape((2, 2, 272, 128), F32), shape((2, 32, 128), F32), shape((8, 128), F32),
        ),
        (mate, far, res_left, res_right, peak0, peak1, stencil),
        stencil=6,
    )
    slab = shape((1344, 128), I16)
    common = (flow, fhigh, sides, parity, tops, codes, hleft, hright, stencil)
    smoothed1, down1, up1, ahead = call(
        functools.partial(complete_kernel, 1, z_count),
        (cube, slab, slab, shape((2064, 128), I16)),
        (smoothed1, *common),
        stencil=9,
    )
    high1 = ring(down1, "gz", -1)
    low1 = ring(up1, "gz", 1)
    earlier = ring(ahead, "phase", 1)
    smoothed0, down0, up0 = call(
        functools.partial(complete_kernel, 0, z_count),
        (cube, slab, slab),
        (smoothed0, *common),
        stencil=9,
    )
    high0 = ring(down0, "gz", -1)
    low0 = ring(up0, "gz", 1)

    def scratch_of(rows, tiles, width):
        return [
            pltpu.VMEM((BS, 128), F32),
            pltpu.VMEM((BS, 128), F32),
            pltpu.VMEM((3, BS, 128), F32),
            pltpu.VMEM((BS, 128, 128), I16),
            pltpu.VMEM((rows, 512, 128), BF16),
            pltpu.VMEM((tiles, width, 256), BF16),
        ]

    partial0, partial1 = call(
        inner_kernel,
        (cube, cube),
        (smoothed0, smoothed1, mask_in, weights_in),
        [pltpu.VMEM((16, 512, 128), BF16)],
    )
    vmem = pl.BlockSpec(memory_space=pltpu.VMEM)
    smem = pl.BlockSpec(memory_space=pltpu.SMEM)
    anywhere = pl.BlockSpec(memory_space=pl.ANY)
    out = ()
    for p, partial, low, high in ((1, partial1, low1, high1), (0, partial0, low0, high0)):
        more = () if p == 1 else (earlier, out)
        out = call(
            functools.partial(outer_kernel, p, z_count, y_count),
            shape(volume.shape, F32),
            (partial, low, high, hleft, hright, left, right, stencil, *more),
            scratch_of(12, 4, 1280),
            grid=(1,),
            in_specs=[vmem] * 7 + [smem] + ([vmem, anywhere] if more else []),
            out_specs=pl.BlockSpec((1,) + volume.shape[1:], functools.partial(phase_block, p)),
            input_output_aliases={9: 0} if more else {},
        )
    return out


def phase_block(p, step):
    return p, 0, 0, 0


def solution(mesh):
    placed = (
        P("phase", None, "gz", "gy"),
        P("phase", "gz", "gy", None),
        P("phase", "gz", "gy", None),
        P(),
    )
    return jax.shard_map(
        body, mesh=mesh, in_specs=placed, out_specs=P("phase", None, "gz", "gy"), check_vma=False
    )
```
